128 devices in a mesh: gx: 32 (over z, y_lo, x), gy: 4 (over y_hi, core).
Axes of the slice: x: 4, y: 4 (y_hi: 2, y_lo: 2; y = y_hi * 2 + y_lo), z: 4, core: 2. Of those that a mesh axis runs over, the one named last changes fastest.
Arguments:
- fluid_source: float32 [256, 128, 512], P('gx', 'gy'), may hold values from -6 to 6
- fluid_diag: float32 [256, 128, 512], P('gx', 'gy'), may hold values from 0.05 to 2
- stiff_ref: float32 [81, 81], replicated
- elem_coef: float32 [49152], P(('gx', 'gy')), may hold values from 0.3 to 3
- connect: int32 [27, 49152], P(None, ('gx', 'gy')), may hold values from 0 to 12543
- live_count: int32 [128], P(('gx', 'gy')), may hold values from 48 to 384, as said below
- node_mass: float32 [393216], P(('gx', 'gy')), may hold values from 0.5 to 2
- solid_load: float32 [3, 393216], P(None, ('gx', 'gy')), may hold values from -24 to 24
- wet_normal: float32 [3, 32768], P(None, ('gx', 'gy')), may hold values from -6 to 6
- trac_face: int32 [4, 32768], P(None, ('gx', 'gy')), may hold values from 0 to 1023
- trac_weight: float32 [4, 32768], P(None, ('gx', 'gy')), may hold values from 0 to 0.5
- wall_node: int32 [4, 256, 128], P(None, 'gx', 'gy'), may hold values from 0 to 1023
- wall_weight: float32 [4, 256, 128], P(None, 'gx', 'gy'), may hold values from 0 to 0.5
Outputs:
- pressure: float32 [256, 128, 512], P('gx', 'gy')
- displacement: float32 [3, 393216], P(None, ('gx', 'gy'))
The draws below stay inside these ranges and needn't reach their ends.
Inputs may be any that keep to these rules, and one draw needn't show every extreme that they name: `connect`: entries number columns of the extended node list of the element's segment: its 12288 own nodes, then the first 256 nodes of the next segment. `live_count`: live slots of each device come first in its 384 slots; some device is full. `trac_face`: indices into the wall faces of the node's span slab, in the order of wall_seg. `wall_node`: indices into the face's segment's list of 1024 wetted nodes.
All inputs are finite; a program needn't handle non-finite values.
Results may differ from the reference program's by a relative error of at most 0.00014.
Values sent between devices are 32-bit elements; how exact they have to be, the bound alone decides.
No kernel may reach another device: no remote copies, remote signals or barrier semaphores. Data moves between devices by JAX's collectives and lax.ppermute only.
A program may use at most 64 MiB of HBM per device.

```python
import math
import jax
import jax.numpy as jnp
from jax import lax

CX = 8
CY = 32
FZ = 512
WET_DEV = 256
PLANE = 256
NPE = 27
ITERS = 2
PSEUDO = 2
COUPLE = 2
DOF = 81
EL_DEV = 384
NS_DEV = 3072
SEG_NODES = 12288
WET_SEG = 1024
FX = 256
FY = 128
NODES = 393216
WET = 32768
ELEMS = 49152
N_GX = 32
N_GY = 4
DEVICES = 128


def draw_stiff_ref(key, part):
    factor_raw = jax.random.uniform(key, (DOF, DOF), jnp.float32, -1.0, 1.0)
    gram = jnp.dot(factor_raw.T, factor_raw, precision=lax.Precision.HIGHEST, preferred_element_type=jnp.float32) / 27.0
    gram = 0.5 * (gram + gram.T)
    return (gram + 0.15 * jnp.eye(DOF, dtype=jnp.float32)).astype(jnp.float32)


def draw_live_count(key, part):
    first_key, second_key = jax.random.split(key)
    level_drawn = jax.random.randint(first_key, (DEVICES,), 0, 1024)
    lowest = EL_DEV // 8
    counts_drawn = lowest + (EL_DEV - lowest) * (level_drawn * level_drawn // 1024) // 1024
    fullest = jax.random.randint(second_key, (), 0, DEVICES)
    return jnp.where(jnp.arange(DEVICES) == fullest, EL_DEV, counts_drawn).astype(jnp.int32)


def with_ends(array, own_key, low, high):
    place = [jax.random.randint(jax.random.fold_in(own_key, axis), (), 0, length) for axis, length in enumerate(array.shape)]
    longest = array.shape.index(max(array.shape))
    next_to = place[:longest] + [(place[longest] + 1) % array.shape[longest]] + place[longest + 1:]
    return array.at[tuple(place)].set(low).at[tuple(next_to)].set(high)


def block_scale(own_key, shape, cuts, low, top_value):
    gain, own = 1.0, jax.random.fold_in(own_key, 6)
    for axis_at, blocks in cuts:
        draws = jnp.exp(jax.random.uniform(jax.random.fold_in(own, axis_at), (blocks,), jnp.float32, low / len(cuts), top_value / len(cuts)))
        gain = gain * jnp.repeat(draws, shape[axis_at] // blocks).reshape([-1 if axis == axis_at else 1 for axis in range(len(shape))])
    return gain


def scatter_about(own_key, shape, scale, bound, shards=(), held_as=jnp.bfloat16):
    entries = scale * jax.random.normal(own_key, shape, jnp.float32)
    if shards:
        entries = entries * block_scale(own_key, shape, shards, -0.22, 0.18)
    return jnp.clip(entries, -bound, bound).astype(held_as)


def setup_inputs(seed: int = 0) -> dict:
    splits = jax.random.split(jax.random.key(seed), 14)
    return {
        "fluid_source": scatter_about(splits[0], (FX, FY, FZ), 1.0, 6.0, ((0, 32), (1, 4)), jnp.float32),
        "fluid_diag": jnp.clip(jnp.exp(math.log(2.0) - 3.6888794 * jax.random.uniform(splits[1], (FX, FY, FZ), jnp.float32) ** block_scale(splits[1], (FX, FY, FZ), ((0, 32), (1, 4)), -0.2, 0.2)), 0.05, 2.0),
        "stiff_ref": draw_stiff_ref(jax.random.fold_in(splits[13], 71), 0),
        "elem_coef": jnp.clip(jnp.exp(math.log(3.0) - 2.3025851 * jax.random.uniform(splits[3], (ELEMS,), jnp.float32) ** block_scale(splits[3], (ELEMS,), ((0, 128),), -0.2, 0.2)), 0.3, 3.0),
        "connect": with_ends(jax.random.randint(splits[4], (NPE, ELEMS), 0, SEG_NODES + PLANE), jax.random.fold_in(splits[4], 1), 0, (SEG_NODES + PLANE) - 1).astype(jnp.int32),
        "live_count": draw_live_count(jax.random.fold_in(splits[13], 71), 0),
        "node_mass": jnp.clip(jnp.exp(math.log(2.0) - 1.3862944 * jax.random.uniform(splits[6], (NODES,), jnp.float32) ** block_scale(splits[6], (NODES,), ((0, 128),), -0.2, 0.2)), 0.5, 2.0),
        "solid_load": scatter_about(splits[7], (3, NODES), 4.0, 24.0, ((1, 128),), jnp.float32),
        "wet_normal": scatter_about(splits[8], (3, WET), 1.0, 6.0, ((1, 128),), jnp.float32),
        "trac_face": with_ends(jax.random.randint(splits[9], (4, WET), 0, CX * FY), jax.random.fold_in(splits[9], 1), 0, (CX * FY) - 1).astype(jnp.int32),
        "trac_weight": jnp.clip(0.5 * jax.random.uniform(splits[10], (4, WET), jnp.float32) ** block_scale(splits[10], (4, WET), ((1, 128),), -0.2, 0.2), 0.0, 0.5),
        "wall_node": with_ends(jax.random.randint(splits[11], (4, FX, FY), 0, WET_SEG), jax.random.fold_in(splits[11], 1), 0, WET_SEG - 1).astype(jnp.int32),
        "wall_weight": jnp.clip(0.5 * jax.random.uniform(splits[12], (4, FX, FY), jnp.float32) ** block_scale(splits[12], (4, FX, FY), ((1, 32), (2, 4)), -0.2, 0.2), 0.0, 0.5),
    }


pseudo_weight = 0.8
traction_scale = 30.0
motion_scale = 2.0
relax_weight = 0.5


def fluid_step(pressure, fluid_diag, forcing):
    padded = jnp.pad(pressure, 1)
    beside = padded[2:, 1:-1, 1:-1] + padded[:-2, 1:-1, 1:-1]
    beside = beside + padded[1:-1, 2:, 1:-1] + padded[1:-1, :-2, 1:-1]
    beside = beside + padded[1:-1, 1:-1, 2:] + padded[1:-1, 1:-1, :-2]
    center = 6.0 + fluid_diag
    applied = center * pressure - beside
    return pressure + pseudo_weight * (forcing - applied) / center


def solid_apply(vector_in, stiff_ref, conn_seg, weight_seg, node_mass):
    seg_nodes = NS_DEV * N_GY
    segments = vector_in.reshape(3, N_GX, seg_nodes).transpose(1, 0, 2)
    following = jnp.concatenate([segments[1:, :, :PLANE], jnp.zeros((1, 3, PLANE), jnp.float32)], axis=0)
    extended = jnp.concatenate([segments, following], axis=2)

    def one_segment(operands):
        ext_nodes, columns, elem_weight = operands
        gathered = ext_nodes[:, columns].reshape(3 * NPE, columns.shape[1])
        product = jnp.dot(stiff_ref, gathered, precision=lax.Precision.HIGHEST, preferred_element_type=jnp.float32)
        product = product * elem_weight[None, :]
        return jnp.zeros_like(ext_nodes).at[:, columns].add(product.reshape(3, NPE, columns.shape[1]))

    summed = lax.map(one_segment, (extended, conn_seg, weight_seg))
    owned_part = summed[:, :, :seg_nodes]
    carried = jnp.concatenate([jnp.zeros((1, 3, PLANE), jnp.float32), summed[:-1, :, seg_nodes:]], axis=0)
    owned_part = owned_part.at[:, :, :PLANE].add(carried)
    return owned_part.transpose(1, 0, 2).reshape(3, -1) + node_mass[None, :] * vector_in


def conjugate(solid_force, apply_fn):
    solution = jnp.zeros_like(solid_force)
    residual = solid_force
    direction = solid_force
    norm_now = jnp.sum(residual * residual)
    for iteration in range(ITERS):
        applied = apply_fn(direction)
        step_size = norm_now / jnp.sum(direction * applied)
        solution = solution + step_size * direction
        residual = residual - step_size * applied
        norm_next = jnp.sum(residual * residual)
        direction = residual + (norm_next / norm_now) * direction
        norm_now = norm_next
    return solution


def reference(fluid_source, fluid_diag, stiff_ref, elem_coef, connect, live_count, node_mass, solid_load, wet_normal, trac_face, trac_weight, wall_node, wall_weight):
    seg_elems = EL_DEV * N_GY
    position = jnp.arange(EL_DEV * DEVICES, dtype=jnp.int32) % EL_DEV
    live_each = jnp.repeat(live_count, EL_DEV)
    elem_weight = elem_coef * (position < live_each).astype(jnp.float32)
    conn_seg = connect.reshape(NPE, N_GX, seg_elems).transpose(1, 0, 2)
    weight_seg = elem_weight.reshape(N_GX, seg_elems)

    def apply_fn(vector_in):
        return solid_apply(vector_in, stiff_ref, conn_seg, weight_seg, node_mass)

    wet_segment = jnp.arange(WET_DEV * DEVICES, dtype=jnp.int32) // (WET_DEV * N_GY)
    row_segment = jnp.arange(CX * N_GX, dtype=jnp.int32) // CX
    pressure = jnp.zeros(fluid_source.shape, jnp.float32)
    displacement = jnp.zeros(solid_load.shape, jnp.float32)
    for coupling in range(COUPLE):
        wet_disp = displacement.reshape(3, DEVICES, NS_DEV)[:, :, :WET_DEV].reshape(3, -1)
        motion = jnp.sum(wet_normal * wet_disp, axis=0).reshape(N_GX, WET_DEV * N_GY)
        picked = motion[row_segment[None, :, None], wall_node]
        wall_source = motion_scale * jnp.sum(wall_weight * picked, axis=0)
        forcing = fluid_source.at[:, :, 0].add(wall_source)
        for pseudo_step in range(PSEUDO):
            pressure = fluid_step(pressure, fluid_diag, forcing)
        wall_seg = pressure[:, :, 0].reshape(N_GX, CX, N_GY, CY).transpose(0, 2, 1, 3).reshape(N_GX, -1)
        traction = jnp.sum(trac_weight * wall_seg[wet_segment[None, :], trac_face], axis=0)
        load_parts = solid_load.reshape(3, DEVICES, NS_DEV)
        pushed = traction_scale * traction.reshape(1, DEVICES, WET_DEV) * wet_normal.reshape(3, DEVICES, WET_DEV)
        solid_force = load_parts.at[:, :, :WET_DEV].add(pushed).reshape(3, -1)
        solution = conjugate(solid_force, apply_fn)
        displacement = displacement + relax_weight * (solution - displacement)
    return pressure, displacement
```

```python
import functools

import jax
import jax.numpy as jnp
from jax import lax
from jax.experimental import pallas as pl
from jax.experimental.pallas import tpu as pltpu
from jax.sharding import PartitionSpec as P

F32 = jnp.float32
BF = jnp.bfloat16
AXES = ("gx", "gy")
N_GX = 32
N_DEV = 128
LR = 64
VR = 56
OWN = 48
CORE = 1
YHI = 2

pseudo_weight = 0.8
traction_scale = 30.0
motion_scale = 2.0
relax_weight = 0.5

VM = pl.BlockSpec(memory_space=pltpu.VMEM)
SM = pl.BlockSpec(memory_space=pltpu.SMEM)


def params(mib=40):
    return pltpu.CompilerParams(vmem_limit_bytes=mib << 20)


def swap(x, mask):
    return lax.ppermute(x, AXES, [(i, i ^ mask) for i in range(N_DEV)])


def from_gx(x, by):
    return lax.ppermute(x, "gx", [(i, i + by) for i in range(N_GX) if 0 <= i + by < N_GX])


def from_gy(x, by):
    return lax.ppermute(x, "gy", [(i, i + by) for i in range(4) if 0 <= i + by < 4])


def split(v):
    hi = v.astype(BF)
    return hi, (v - hi.astype(F32)).astype(BF)


def apply_body(nblk_ref, v_ref, conn_ref, ew_ref, s_ref, out_ref, t_scr, oh_scr, ml_scr, x_scr, a_scr, acc):
    for c in range(3):
        v = jnp.concatenate([v_ref[c], jnp.zeros((LR - VR, 256), F32)], axis=0)
        hi, lo = split(v)
        t_scr[c * LR : (c + 1) * LR, 0:256] = hi
        t_scr[c * LR : (c + 1) * LR, 256:512] = lo
    acc[...] = jnp.zeros_like(acc)
    i256 = lax.broadcasted_iota(jnp.int32, (256, 128), 0)
    i64 = lax.broadcasted_iota(jnp.int32, (LR, 128), 0)

    def block(b, carry):
        for p in range(14):
            for h in range(2):
                k = 2 * p + h
                sl = slice(p * 256 + h * 128, p * 256 + h * 128 + 128)
                if k == 27:
                    oh_scr[:, sl] = jnp.zeros((256, 128), BF)
                    ml_scr[:, sl] = jnp.zeros((LR, 128), BF)
                    a_scr[:, sl] = jnp.zeros((384, 128), BF)
                    continue
                idx = conn_ref[b, k : k + 1, :]
                oh_scr[:, sl] = (i256 == (idx & 255)).astype(F32).astype(BF)
                ml_scr[:, sl] = (i64 == (idx >> 8)).astype(F32).astype(BF)
            sp = slice(p * 256, p * 256 + 256)
            oh = oh_scr[:, sp]
            g = jnp.dot(t_scr[...], jnp.concatenate([oh, oh], axis=0), preferred_element_type=F32)
            m = ml_scr[:, sp].astype(F32)
            for c in range(3):
                s = (g[c * LR : (c + 1) * LR] * m).reshape(8, 8, 256).sum(axis=0)
                for h in range(2):
                    k = 2 * p + h
                    if k < 27:
                        x_scr[k * 24 + c * 8 : k * 24 + c * 8 + 8, :] = s[:, h * 128 : h * 128 + 128]
        xh, xl = split(x_scr[...])
        r = jnp.dot(s_ref[...], xh, preferred_element_type=F32)
        prod = r[:88] + r[88:] + jnp.dot(s_ref[0:88, :], xl, preferred_element_type=F32)
        prod = prod * ew_ref[b]
        ph = prod.astype(BF).astype(F32)
        parts = (ph, prod - ph)
        for k in range(27):
            sl = slice(k * 128, k * 128 + 128)
            m = ml_scr[:, sl].reshape(4, 16, 128)
            for c in range(3):
                row = c * 27 + k
                for j, src in enumerate(parts):
                    r16 = jnp.broadcast_to(src[row : row + 1, :], (16, 128)).astype(BF)
                    at = j * 192 + c * LR
                    a_scr[at : at + LR, sl] = (m * r16[None]).reshape(LR, 128)
        acc[...] += lax.dot_general(
            a_scr[...], oh_scr[...], (((1,), (1,)), ((), ())), preferred_element_type=F32
        )
        return carry

    lax.fori_loop(0, nblk_ref[0], block, 0)
    for c in range(3):
        s = acc[c * LR : (c + 1) * LR, :] + acc[192 + c * LR : 192 + (c + 1) * LR, :]
        out_ref[c] = s[:VR]


def stiff_apply(nblk, v, conn, ew, s):
    return pl.pallas_call(
        apply_body,
        out_shape=jax.ShapeDtypeStruct((3, VR, 256), F32),
        in_specs=[SM] + [VM] * 4,
        out_specs=VM,
        scratch_shapes=[
            pltpu.VMEM((192, 512), BF),
            pltpu.VMEM((256, 3584), BF),
            pltpu.VMEM((LR, 3584), BF),
            pltpu.VMEM((648, 128), F32),
            pltpu.VMEM((384, 3584), BF),
            pltpu.VMEM((384, 256), F32),
        ],
        compiler_params=params(),
    )(nblk, v, conn, ew, s)


def prep_stiff(stiff):
    e = jnp.repeat(stiff.reshape(81, 3, 27).transpose(0, 2, 1).reshape(81, 81), 8, axis=1)
    e = jnp.concatenate([e, jnp.zeros((7, 648), F32)], axis=0)
    h = lax.reduce_precision(e, 8, 7)
    return jnp.concatenate([h.astype(BF), (e - h).astype(BF)], axis=0)


def finish_body(at_ref, p_ref, q_ref, mass_ref, v_ref, w_ref, dots_ref, *, second):
    keep = lax.broadcasted_iota(jnp.int32, (VR, 256), 0)
    live = jnp.where(at_ref[0] == N_GX - 1, OWN, OWN + 1)
    mask = (keep < live).astype(F32)
    dots = [jnp.zeros((8, 256), F32) for _ in range(3)]
    for c in range(3):
        v = v_ref[c]
        w = (p_ref[c] + q_ref[c] + mass_ref[...] * v) * mask
        w_ref[c] = w
        pairs = ((v, w),) if second else ((v, v), (v, w), (w, w))
        for i, (x, y) in enumerate(pairs):
            dots[i] = dots[i] + (x[:OWN] * y[:OWN]).reshape(6, 8, 256).sum(axis=0)
    rows = [d.sum(axis=0, keepdims=True) for d in dots]
    rows = [d[:, :128] + d[:, 128:] for d in rows]
    dots_ref[...] = jnp.concatenate(rows + [jnp.zeros((5, 128), F32)], axis=0)


def finish(at, p, q, mass, v, second):
    return pl.pallas_call(
        functools.partial(finish_body, second=second),
        out_shape=(jax.ShapeDtypeStruct((3, VR, 256), F32), jax.ShapeDtypeStruct((8, 128), F32)),
        in_specs=[SM] + [VM] * 4,
        out_specs=(VM, VM),
        compiler_params=params(),
    )(at, p, q, mass, v)


def rows_in(at_ref):
    x = lax.broadcasted_iota(jnp.int32, (16, 128), 0) + at_ref[0] * 8 - 3
    return ((x >= 0) & (x < N_GX * 8)).astype(F32)


def wall_step(p, gain, force, inside, depth):
    lane = lax.broadcasted_iota(jnp.int32, (16, 128), 1)
    out = []
    for z in range(depth):
        c = p[z]
        n = pltpu.roll(c, 1, 0) + pltpu.roll(c, 15, 0)
        n = n + jnp.where(lane == 0, 0.0, pltpu.roll(c, 1, 1))
        n = n + jnp.where(lane == 127, 0.0, pltpu.roll(c, 127, 1))
        n = n + p[z + 1]
        if z > 0:
            n = n + p[z - 1]
        out.append(((1.0 - pseudo_weight) * c + gain[z] * (force[z] + n)) * inside)
    return out


def wall_front(at_ref, slab_ref):
    inside = rows_in(at_ref)
    fs = [slab_ref[z * 16 : z * 16 + 16, :] for z in range(4)]
    gain = [pseudo_weight / (6.0 + slab_ref[64 + z * 16 : 64 + z * 16 + 16, :]) for z in range(4)]
    p1 = [gain[z] * fs[z] * inside for z in range(4)]
    p2 = wall_step(p1, gain, fs, inside, 3)
    return inside, fs, gain, p2


def push(wall16, load_ref, seg_ref, f_ref):
    wall = pltpu.roll(wall16, 13, 0)[0:8]
    hi, lo = split(wall)
    table = jnp.concatenate([hi, lo], axis=0)
    i128 = lax.broadcasted_iota(jnp.int32, (128, 256), 0)
    i8 = lax.broadcasted_iota(jnp.int32, (8, 256), 0)
    f_ref[...] = load_ref[...]
    for g in range(4):
        total = jnp.zeros((8, 256), F32)
        for k in range(4):
            face = seg_ref[g, k : k + 1, :].astype(jnp.int32)
            oh = (i128 == ((face >> 8) * 32 + (face & 31))).astype(F32).astype(BF)
            r = jnp.dot(table, oh, preferred_element_type=F32)
            w = jnp.where(i8 == ((face >> 5) & 7), seg_ref[g, 4 + k : 5 + k, :], 0.0)
            total = total + (r[:8] + r[8:]) * w
        traction = total.sum(axis=0, keepdims=True)
        for c in range(3):
            f_ref[c, 12 * g : 12 * g + 1, :] = (
                f_ref[c, 12 * g : 12 * g + 1, :]
                + traction_scale * traction * seg_ref[g, 8 + c : 9 + c, :]
            )


def first_body(at_ref, slab_ref, load_ref, seg_ref, f_ref):
    inside, fs, gain, p2 = wall_front(at_ref, slab_ref)
    push(p2[0], load_ref, seg_ref, f_ref)


def first_force(at, slab, load, seg):
    return pl.pallas_call(
        first_body,
        out_shape=jax.ShapeDtypeStruct((3, VR, 256), F32),
        in_specs=[SM, VM, VM, VM],
        out_specs=VM,
        compiler_params=params(),
    )(at, slab, load, seg)


def second_body(at_ref, slab_ref, load_ref, seg_ref, ws_ref, f_ref):
    inside, fs, gain, p2 = wall_front(at_ref, slab_ref)
    force = [fs[0] + ws_ref[...], fs[1]]
    p3 = wall_step(p2, gain, force, inside, 2)
    p4 = wall_step(p3, gain, force, inside, 1)
    push(p4[0], load_ref, seg_ref, f_ref)


def second_force(at, slab, load, seg, ws):
    return pl.pallas_call(
        second_body,
        out_shape=jax.ShapeDtypeStruct((3, VR, 256), F32),
        in_specs=[SM] + [VM] * 4,
        out_specs=VM,
        compiler_params=params(),
    )(at, slab, load, seg, ws)


def weights_of(sums):
    a, b, c, d = [sums[i : i + 1, :].sum(axis=1, keepdims=True) for i in range(4)]
    alpha = a / b
    beta = (c - b * (b / a)) / (d - c * (c / b))
    return alpha + beta * (alpha * (c / b)), -alpha * beta


def source_body(sums_ref, inv_ref, f_ref, w_ref, seg_ref, pick_ref, ws_ref):
    c0, c1 = weights_of(sums_ref[...])
    c0, c1 = c0 * inv_ref[0], c1 * inv_ref[0]
    rows = []
    for g in range(4):
        total = jnp.zeros((1, 256), F32)
        for c in range(3):
            sl = slice(12 * g, 12 * g + 1)
            disp = relax_weight * (c0 * f_ref[c, sl, :] + c1 * w_ref[c, sl, :])
            total = total + seg_ref[g, 8 + c : 9 + c, :] * disp
        rows.append(total)
    hi, lo = split(jnp.concatenate(rows + [jnp.zeros((4, 256), F32)], axis=0))
    table = jnp.concatenate([hi, lo], axis=0)
    i256 = lax.broadcasted_iota(jnp.int32, (256, 128), 0)
    i8 = lax.broadcasted_iota(jnp.int32, (8, 128), 0)
    for x in range(8):
        total = jnp.zeros((8, 128), F32)
        for k in range(4):
            at = k * 8 + x
            node = pick_ref[at : at + 1, :].astype(jnp.int32)
            oh = (i256 == (node & 255)).astype(F32).astype(BF)
            r = jnp.dot(table, oh, preferred_element_type=F32)
            w = jnp.where(i8 == (node >> 8), pick_ref[32 + at : 33 + at, :], 0.0)
            total = total + (r[:8] + r[8:]) * w
        ws_ref[x : x + 1, :] = motion_scale * total.sum(axis=0, keepdims=True)


def wall_source(sums, inv, f, w, seg, pick):
    return pl.pallas_call(
        source_body,
        out_shape=jax.ShapeDtypeStruct((8, 128), F32),
        in_specs=[VM, SM] + [VM] * 4,
        out_specs=VM,
        compiler_params=params(),
    )(sums, inv, f, w, seg, pick)


def fluid_body(at_ref, fs_ref, fd_ref, xlo_ref, xhi_ref, ylo_ref, yhi_ref, ws_ref, out_ref, src, gain, pa, pb):
    for j, (ref, dst) in enumerate(((fs_ref, src), (fd_ref, gain))):
        for x in range(14):
            if x < 3:
                own = xlo_ref[j, x]
            elif x < 11:
                own = ref[x - 3]
            else:
                own = xhi_ref[j, x - 11]
            dst[x, 8:40, :] = own
            dst[x, 0:8, :] = ylo_ref[j, x]
            dst[x, 40:48, :] = yhi_ref[j, x]
    lane = lax.broadcasted_iota(jnp.int32, (48, 512), 1)
    y = lax.broadcasted_iota(jnp.int32, (48, 512), 0) + at_ref[1] * 32 - 8
    y_in = ((y >= 0) & (y < 128)).astype(F32)

    def x_in(x):
        gx = at_ref[0] * 8 + x - 3
        return jnp.where((gx >= 0) & (gx < N_GX * 8), 1.0, 0.0).astype(F32)

    def start(x, carry):
        g = pseudo_weight / (6.0 + gain[x]) * (y_in * x_in(x))
        gain[x] = g
        pa[x] = g * src[x]
        return carry

    lax.fori_loop(0, 14, start, 0)

    def new_row(p, x):
        c = p[x]
        n = p[x - 1] + p[x + 1] + pltpu.roll(c, 1, 0) + pltpu.roll(c, 47, 0)
        n = n + jnp.where(lane == 0, 0.0, pltpu.roll(c, 1, 1))
        n = n + jnp.where(lane == 511, 0.0, pltpu.roll(c, 511, 1))
        return (1.0 - pseudo_weight) * c + gain[x] * (src[x] + n)

    def second(x, carry):
        pb[x] = new_row(pa, x)
        return carry

    lax.fori_loop(1, 13, second, 0)

    def add_source(x, carry):
        src[x, :, 0:128] = src[x, :, 0:128] + ws_ref[x]
        return carry

    lax.fori_loop(2, 12, add_source, 0)

    def third(x, carry):
        pa[x] = new_row(pb, x)
        return carry

    lax.fori_loop(2, 12, third, 0)

    def fourth(x, carry):
        out_ref[x - 3] = new_row(pa, x)[8:40]
        return carry

    lax.fori_loop(3, 11, fourth, 0)


def fluid(at, fs, fd, xlo, xhi, ylo, yhi, ws):
    return pl.pallas_call(
        fluid_body,
        out_shape=jax.ShapeDtypeStruct((8, 32, 512), F32),
        in_specs=[SM] + [VM] * 7,
        out_specs=VM,
        scratch_shapes=[pltpu.VMEM((14, 48, 512), F32)] * 4,
        compiler_params=params(),
    )(at, fs, fd, xlo, xhi, ylo, yhi, ws)


def last_body(s1_ref, s2_ref, inv_ref, f1_ref, w1_ref, f2_ref, w2_ref, out_ref):
    c0, c1 = weights_of(s1_ref[...])
    d0, d1 = weights_of(s2_ref[...])
    inv = inv_ref[0]
    c0, c1, d0, d1 = c0 * inv, c1 * inv, d0 * inv, d1 * inv
    for c in range(3):
        before = relax_weight * (c0 * f1_ref[c] + c1 * w1_ref[c])
        solved = d0 * f2_ref[c] + d1 * w2_ref[c]
        out_ref[c] = before + relax_weight * (solved - before)


def last(s1, s2, inv, f1, w1, f2, w2):
    return pl.pallas_call(
        last_body,
        out_shape=jax.ShapeDtypeStruct((3, 12, 256), F32),
        in_specs=[VM, VM, SM] + [VM] * 4,
        out_specs=VM,
        compiler_params=params(),
    )(s1, s2, inv, f1, w1, f2, w2)


def local(
    fluid_source,
    fluid_diag,
    stiff_ref,
    elem_coef,
    connect,
    live_count,
    node_mass,
    solid_load,
    wet_normal,
    trac_face,
    trac_weight,
    wall_node,
    wall_weight,
):
    gx = lax.axis_index("gx")
    gy = lax.axis_index("gy")
    core = gy & 1
    yhi = gy >> 1
    at = jnp.stack([gx, gy]).astype(jnp.int32)

    def by_core(own, other, axis):
        lo = jnp.where(core == 0, own, other)
        hi = jnp.where(core == 0, other, own)
        return jnp.concatenate([lo, hi], axis=axis)

    def by_yhi(own, other, axis):
        lo = jnp.where(yhi == 0, own, other)
        hi = jnp.where(yhi == 0, other, own)
        return jnp.concatenate([lo, hi], axis=axis)

    def gather(x, axis):
        pair = by_core(x, swap(x, CORE), axis)
        return by_yhi(pair, swap(pair, YHI), axis)

    layers = jnp.stack([fluid_source[:, :, :4], fluid_diag[:, :, :4]]).transpose(0, 3, 1, 2)
    below = from_gx(layers[:, :, 5:8], 1)
    above = from_gx(layers[:, :, 0:3], -1)
    layers = jnp.concatenate([below, layers, above, jnp.zeros((2, 4, 2, 32), F32)], axis=2)
    picks = jnp.concatenate([wall_node.astype(F32).reshape(32, 32), wall_weight.reshape(32, 32)], axis=0)
    wide = gather(jnp.concatenate([layers.reshape(128, 32), picks], axis=0), 1)
    slab, pick = wide[:128], wide[128:]

    scale = 1.0 / jnp.maximum(1.0, jnp.trace(stiff_ref))
    inv = scale.reshape(1)
    parts = jnp.concatenate(
        [
            solid_load.reshape(36, 256),
            node_mass.reshape(12, 256) * scale,
            trac_face.astype(F32),
            trac_weight,
            wet_normal,
        ],
        axis=0,
    )
    parts = gather(parts[None], 0)
    load = jnp.concatenate(
        [parts[:, :36].reshape(4, 3, 12, 256).transpose(1, 0, 2, 3).reshape(3, OWN, 256), jnp.zeros((3, VR - OWN, 256), F32)],
        axis=1,
    )
    mass = parts[:, 36:48].reshape(OWN, 256)
    mass_next = from_gx(mass[0:1], -1)
    mass = jnp.concatenate([mass, mass_next, jnp.zeros((VR - OWN - 1, 256), F32)], axis=0)
    seg = jnp.concatenate([parts[:, 48:59], jnp.zeros((4, 5, 256), F32)], axis=1)

    stiff = prep_stiff(stiff_ref * scale)
    conn = connect.reshape(27, 3, 128).transpose(1, 0, 2)
    live = live_count[0]
    nblk = ((live + 127) // 128).reshape(1)
    position = jnp.arange(384, dtype=jnp.int32)
    ew = (elem_coef * (position < live).astype(F32)).reshape(3, 1, 128)

    row = lax.broadcasted_iota(jnp.int32, (3, VR, 256), 1)

    def with_plane(f):
        following = from_gx(f[:, 0, :], -1)
        return jnp.where(row == OWN, following[:, None, :], f)

    def apply_fn(v, second):
        s = stiff_apply(nblk, v, conn, ew, stiff)
        tail = from_gx(s[:, OWN, :], 1)
        head = from_gx(s[:, 0, :], -1)
        s = s + jnp.where(row == 0, tail[:, None, :], 0.0) + jnp.where(row == OWN, head[:, None, :], 0.0)
        pair = s + swap(s, CORE)
        return finish(at, pair, swap(pair, YHI), mass, v, second)

    def total(x):
        for mask in (1, 3, 4, 8, 24):
            x = x + swap(x, mask * 4)
        return x

    def solve(f):
        w, dots = apply_fn(f, False)
        _, more = apply_fn(w, True)
        return w, total(jnp.concatenate([dots[0:3], more[0:1], jnp.zeros((4, 128), F32)], axis=0))

    f1 = with_plane(first_force(at, slab, load, seg))
    w1, s1 = solve(f1)
    ws = wall_source(s1, inv, f1, w1, seg, pick)
    ws_lo = from_gx(ws[7:8], 1)
    ws_hi = from_gx(ws[0:1], -1)
    ws = jnp.concatenate([jnp.zeros((2, 128), F32), ws_lo, ws, ws_hi, jnp.zeros((4, 128), F32)], axis=0)
    f2 = with_plane(second_force(at, slab, load, seg, ws))
    w2, s2 = solve(f2)

    def mine(x):
        return lax.dynamic_slice_in_dim(x, gy * 12, 12, axis=1)

    displacement = last(s1, s2, inv, mine(f1), mine(w1), mine(f2), mine(w2)).reshape(3, 3072)

    both = jnp.stack([fluid_source, fluid_diag])
    xlo = from_gx(both[:, 5:8], 1)
    xhi = from_gx(both[:, 0:3], -1)
    tall = jnp.concatenate([xlo, both, xhi], axis=1)
    ylo = from_gy(tall[:, :, 24:32], 1)
    yhi_block = from_gy(tall[:, :, 0:8], -1)
    padded = jnp.pad(ws, ((0, 0), (8, 8)))
    wall = lax.dynamic_slice_in_dim(padded, gy * 32, 48, axis=1)
    lane = lax.broadcasted_iota(jnp.int32, (16, 48, 128), 2)
    wall = jnp.where(lane == 0, wall[:, :, None], 0.0)
    pressure = fluid(at, fluid_source, fluid_diag, xlo, xhi, ylo, yhi_block, wall)
    return pressure, displacement


def solution(mesh):
    in_specs = (
        P("gx", "gy", None),
        P("gx", "gy", None),
        P(),
        P(("gx", "gy")),
        P(None, ("gx", "gy")),
        P(("gx", "gy")),
        P(("gx", "gy")),
        P(None, ("gx", "gy")),
        P(None, ("gx", "gy")),
        P(None, ("gx", "gy")),
        P(None, ("gx", "gy")),
        P(None, "gx", "gy"),
        P(None, "gx", "gy"),
    )
    out_specs = (P("gx", "gy", None), P(None, ("gx", "gy")))
    return jax.shard_map(local, mesh=mesh, in_specs=in_specs, out_specs=out_specs, check_vma=False)
```

```python
import functools

import jax
import jax.numpy as jnp
from jax import lax
from jax.experimental import pallas as pl
from jax.experimental.pallas import tpu as pltpu
from jax.sharding import PartitionSpec as P

F32 = jnp.float32
BF = jnp.bfloat16
AXES = ("gx", "gy")
N_GX = 32
N_DEV = 128
LR = 64
VR = 56
OWN = 48
CORE = 1
YHI = 2

pseudo_weight = 0.8
traction_scale = 30.0
motion_scale = 2.0
relax_weight = 0.5

VM = pl.BlockSpec(memory_space=pltpu.VMEM)
SM = pl.BlockSpec(memory_space=pltpu.SMEM)


def params(mib=40):
    return pltpu.CompilerParams(vmem_limit_bytes=mib << 20)


def swap(x, mask):
    return lax.ppermute(x, AXES, [(i, i ^ mask) for i in range(N_DEV)])


def from_gx(x, by):
    return lax.ppermute(x, "gx", [(i, i + by) for i in range(N_GX) if 0 <= i + by < N_GX])


def from_gy(x, by):
    return lax.ppermute(x, "gy", [(i, i + by) for i in range(4) if 0 <= i + by < 4])


def split(v):
    hi = v.astype(BF)
    return hi, (v - hi.astype(F32)).astype(BF)


def scale_of(stiff_ref):
    r = lax.broadcasted_iota(jnp.int32, (81, 81), 0)
    c = lax.broadcasted_iota(jnp.int32, (81, 81), 1)
    diag = jnp.where(r == c, stiff_ref[...], 0.0)
    trace = diag.sum(axis=1, keepdims=True).sum(axis=0, keepdims=True)
    return 1.0 / jnp.maximum(1.0, trace)


def fill_stiff(stiff_ref, s_scr):
    s_scr[...] = jnp.zeros_like(s_scr)
    hi, lo = split(jnp.pad(stiff_ref[...] * scale_of(stiff_ref), ((0, 15), (0, 7))))
    s_scr[0:96, :] = hi
    s_scr[96:192, :] = lo


def fill_table(v_ref, t_scr):
    for c in range(3):
        v = jnp.concatenate([v_ref[c], jnp.zeros((LR - VR, 256), F32)], axis=0)
        hi, lo = split(v)
        t_scr[c * LR : (c + 1) * LR, 0:256] = hi
        t_scr[c * LR : (c + 1) * LR, 256:512] = lo


def block_of(b):
    return pl.ds(pl.multiple_of(b * 128, 128), 128)


def forces_of(x, s_scr, coef_ref, live, b):
    xh, xl = split(x)
    r = jnp.dot(s_scr[...], xh, preferred_element_type=F32)
    prod = r[:88] + r[96:184] + jnp.dot(s_scr[0:96, :], xl, preferred_element_type=F32)[:88]
    slot = lax.broadcasted_iota(jnp.int32, (1, 128), 1) + b * 128
    return prod * jnp.where(slot < live, coef_ref[:, block_of(b)], 0.0)


def apply_body(live_ref, v_ref, conn_ref, coef_ref, stiff_ref, out_ref, t_scr, s_scr, oh_scr, ml_scr, x_scr, a_scr, acc):
    fill_table(v_ref, t_scr)
    fill_stiff(stiff_ref, s_scr)
    x_scr[80:88, :] = jnp.zeros((8, 128), F32)
    acc[...] = jnp.zeros_like(acc)
    i256 = lax.broadcasted_iota(jnp.int32, (256, 128), 0)
    i64 = lax.broadcasted_iota(jnp.int32, (LR, 128), 0)
    oh_scr[:, 27 * 128 :] = jnp.zeros((256, 128), BF)
    ml_scr[:, 27 * 128 :] = jnp.zeros((LR, 128), BF)
    a_scr[:, 27 * 128 :] = jnp.zeros((384, 128), BF)
    live = live_ref[0]

    def block(b, carry):
        for p in range(14):
            for h in range(2):
                k = 2 * p + h
                if k < 27:
                    sl = slice(k * 128, k * 128 + 128)
                    idx = conn_ref[k : k + 1, block_of(b)]
                    oh_scr[:, sl] = (i256 == (idx & 255)).astype(F32).astype(BF)
                    ml_scr[:, sl] = (i64 == (idx >> 8)).astype(F32).astype(BF)
            sp = slice(p * 256, p * 256 + 256)
            oh = oh_scr[:, sp]
            g = jnp.dot(t_scr[...], jnp.concatenate([oh, oh], axis=0), preferred_element_type=F32)
            m = ml_scr[:, sp].astype(F32)
            for c in range(3):
                s = (g[c * LR : (c + 1) * LR] * m).sum(axis=0, keepdims=True)
                for h in range(2):
                    k = 2 * p + h
                    if k < 27:
                        x_scr[c * 27 + k : c * 27 + k + 1, :] = s[:, h * 128 : h * 128 + 128]
        prod = forces_of(x_scr[...], s_scr, coef_ref, live, b)
        ph = prod.astype(BF).astype(F32)
        parts = (ph, prod - ph)
        for k in range(27):
            sl = slice(k * 128, k * 128 + 128)
            m = ml_scr[:, sl].reshape(4, 16, 128)
            for c in range(3):
                row = c * 27 + k
                for j, src in enumerate(parts):
                    r16 = jnp.broadcast_to(src[row : row + 1, :], (16, 128)).astype(BF)
                    at = j * 192 + c * LR
                    a_scr[at : at + LR, sl] = (m * r16[None]).reshape(LR, 128)
        acc[...] += lax.dot_general(
            a_scr[...], oh_scr[...], (((1,), (1,)), ((), ())), preferred_element_type=F32
        )
        return carry

    lax.fori_loop(0, (live + 127) // 128, block, 0)
    for c in range(3):
        s = acc[c * LR : (c + 1) * LR, :] + acc[192 + c * LR : 192 + (c + 1) * LR, :]
        out_ref[c] = s[:VR]


def stiff_apply(live, v, conn, coef, stiff):
    return pl.pallas_call(
        apply_body,
        out_shape=jax.ShapeDtypeStruct((3, VR, 256), F32),
        in_specs=[SM] + [VM] * 4,
        out_specs=VM,
        scratch_shapes=[
            pltpu.VMEM((192, 512), BF),
            pltpu.VMEM((192, 88), BF),
            pltpu.VMEM((256, 3584), BF),
            pltpu.VMEM((LR, 3584), BF),
            pltpu.VMEM((88, 128), F32),
            pltpu.VMEM((384, 3584), BF),
            pltpu.VMEM((384, 256), F32),
        ],
        compiler_params=params(),
    )(live, v, conn, coef, stiff)


def pack_parts_body(stiff_ref, load_ref, mass_ref, face_ref, tw_ref, normal_ref, out_ref):
    def put(at, row):
        out_ref[at : at + 1, :] = row[:, :128]
        out_ref[64 + at : 65 + at, :] = row[:, 128:]

    scale = scale_of(stiff_ref)
    for r in range(12):
        sl = slice(r * 256, r * 256 + 256)
        for c in range(3):
            put(c * 12 + r, load_ref[c : c + 1, sl])
        put(36 + r, mass_ref[:, sl] * scale)
    for k in range(4):
        put(48 + k, face_ref[k : k + 1, :].astype(F32))
        put(52 + k, tw_ref[k : k + 1, :])
    for c in range(3):
        put(56 + c, normal_ref[c : c + 1, :])
    zero = jnp.zeros((1, 256), F32)
    for r in range(59, 64):
        put(r, zero)


def pack_parts(stiff, load, mass, face, weight, normal):
    return pl.pallas_call(
        pack_parts_body,
        out_shape=jax.ShapeDtypeStruct((128, 128), F32),
        in_specs=[VM] * 6,
        out_specs=VM,
        compiler_params=params(),
    )(stiff, load, mass, face, weight, normal)


def pack_wall_body(at_ref, fs_ref, fd_ref, xa_ref, xb_ref, node_ref, ww_ref, out_ref):
    out_ref[...] = jnp.zeros_like(out_ref)
    even = jnp.full((32, 128), at_ref[0] & 1, jnp.int32) == 0
    for j, ref in enumerate((fs_ref, fd_ref)):
        for x in range(14):
            if x < 3:
                v = jnp.where(even, xb_ref[j, x], xa_ref[j, x])
            elif x < 11:
                v = ref[x - 3]
            else:
                v = jnp.where(even, xa_ref[j, x - 11], xb_ref[j, x - 11])
            t = v.T
            for z in range(4):
                at = j * 64 + z * 16 + x
                out_ref[at : at + 1, 0:32] = t[z : z + 1, :]
    for k in range(4):
        out_ref[128 + k * 8 : 136 + k * 8, 0:32] = node_ref[k].astype(F32)
        out_ref[160 + k * 8 : 168 + k * 8, 0:32] = ww_ref[k]
    out_ref[...] = pltpu.roll(out_ref[...], at_ref[1] * 32, 1)


def pack_wall(at, fs, fd, xa, xb, node, weight):
    def block(*shape):
        return pl.BlockSpec(shape, lambda i: (0,) * len(shape))

    return pl.pallas_call(
        pack_wall_body,
        grid=(1,),
        out_shape=jax.ShapeDtypeStruct((192, 128), F32),
        in_specs=[
            SM,
            block(8, 32, 128),
            block(8, 32, 128),
            block(2, 3, 32, 128),
            block(2, 3, 32, 128),
            block(4, 8, 32),
            block(4, 8, 32),
        ],
        out_specs=block(192, 128),
        compiler_params=params(),
    )(at, fs, fd, xa, xb, node, weight)


def source_of(vec_ref, seg_ref, pick_ref):
    rows = []
    for g in range(4):
        total = jnp.zeros((1, 256), F32)
        for c in range(3):
            total = total + seg_ref[g, 8 + c : 9 + c, :] * vec_ref[c, 12 * g : 12 * g + 1, :]
        rows.append(total)
    return split(jnp.concatenate(rows + [jnp.zeros((4, 256), F32)], axis=0))


def settle_body(*refs, first):
    at_ref, live_ref, p_ref, q_ref, mass_ref, v_ref, conn_ref, coef_ref, stiff_ref = refs[:9]
    if first:
        seg_ref, pick_ref, w_ref, out_ref, ws_ref = refs[9:14]
    else:
        w_ref, out_ref = refs[9:11]
    t_scr, s_scr, x_scr, acc = refs[-4:]
    keep = lax.broadcasted_iota(jnp.int32, (VR, 256), 0)
    end = jnp.where(at_ref[0] == N_GX - 1, OWN, OWN + 1)
    mask = (keep < end).astype(F32)
    mass = mass_ref[...]
    dots = [jnp.zeros((8, 256), F32) for _ in range(4)]
    for c in range(3):
        v = v_ref[c]
        w = (p_ref[c] + q_ref[c] + mass * v) * mask
        w_ref[c] = w
        for i, (x, y) in enumerate(((v, v), (v, w), (w, w), (w, mass * w))):
            dots[i] = dots[i] + (x[:OWN] * y[:OWN]).reshape(6, 8, 256).sum(axis=0)
    dots = [0.25 * d.sum(axis=0, keepdims=True).sum(axis=1, keepdims=True) for d in dots]

    if first:
        hf, lf = source_of(v_ref, seg_ref, pick_ref)
        hw, lw = source_of(w_ref, seg_ref, pick_ref)
        table = jnp.concatenate([hf, lf, hw, lw], axis=0)
        n256 = lax.broadcasted_iota(jnp.int32, (256, 128), 0)
        n8 = lax.broadcasted_iota(jnp.int32, (8, 128), 0)
        for x in range(8):
            tf = jnp.zeros((8, 128), F32)
            tw = jnp.zeros((8, 128), F32)
            for k in range(4):
                row = k * 8 + x
                node = pick_ref[row : row + 1, :].astype(jnp.int32)
                oh = (n256 == (node & 255)).astype(F32).astype(BF)
                r = jnp.dot(table, oh, preferred_element_type=F32)
                u = jnp.where(n8 == (node >> 8), pick_ref[32 + row : 33 + row, :], 0.0)
                tf = tf + (r[0:8] + r[8:16]) * u
                tw = tw + (r[16:24] + r[24:32]) * u
            ws_ref[x : x + 1, :] = (motion_scale * relax_weight) * tf.sum(axis=0, keepdims=True)
            ws_ref[8 + x : 9 + x, :] = (motion_scale * relax_weight) * tw.sum(axis=0, keepdims=True)

    fill_table(w_ref, t_scr)
    fill_stiff(stiff_ref, s_scr)
    acc[...] = jnp.zeros_like(acc)
    x_scr[80:88, :] = jnp.zeros((8, 128), F32)
    i256 = lax.broadcasted_iota(jnp.int32, (256, 128), 0)
    i64 = lax.broadcasted_iota(jnp.int32, (LR, 128), 0)
    live = live_ref[0]

    def block(b, carry):
        for p in range(14):
            pieces, masks = [], []
            for k in (2 * p, 2 * p + 1):
                idx = conn_ref[min(k, 26) : min(k, 26) + 1, block_of(b)]
                pieces.append((i256 == (idx & 255)).astype(F32).astype(BF))
                masks.append((i64 == (idx >> 8)).astype(F32))
            oh = jnp.concatenate(pieces, axis=1)
            g = jnp.dot(t_scr[...], jnp.concatenate([oh, oh], axis=0), preferred_element_type=F32)
            m = jnp.concatenate(masks, axis=1)
            for c in range(3):
                s = (g[c * LR : (c + 1) * LR] * m).sum(axis=0, keepdims=True)
                for h in range(2):
                    k = 2 * p + h
                    if k < 27:
                        x_scr[c * 27 + k : c * 27 + k + 1, :] = s[:, h * 128 : h * 128 + 128]
        x = x_scr[...]
        acc[...] += (forces_of(x, s_scr, coef_ref, live, b) * x).sum(axis=0, keepdims=True)
        return carry

    lax.fori_loop(0, (live + 127) // 128, block, 0)
    dots[3] = dots[3] + acc[...].sum(axis=1, keepdims=True)
    lane = lax.broadcasted_iota(jnp.int32, (1, 128), 1)
    row = jnp.zeros((1, 128), F32)
    for i in range(4):
        row = jnp.where(lane == i, dots[i], row)
    row = jnp.broadcast_to(row, (N_DEV, 128))
    if first:
        peer = lax.broadcasted_iota(jnp.int32, (N_DEV, 128), 0) >> 2
        after = peer > at_ref[0]
        out_ref[pl.ds(0, N_DEV, 4), :] = row
        out_ref[pl.ds(1, N_DEV, 4), :] = jnp.where(after, ws_ref[7:8, :], ws_ref[0:1, :])
        out_ref[pl.ds(2, N_DEV, 4), :] = jnp.where(after, ws_ref[15:16, :], ws_ref[8:9, :])
        out_ref[pl.ds(3, N_DEV, 4), :] = jnp.zeros((N_DEV, 128), F32)
    else:
        out_ref[...] = row


def settle(at, live, p, q, mass, v, conn, coef, stiff, wall=()):
    first = bool(wall)
    shapes = [(3, VR, 256), (4 * N_DEV, 128), (16, 128)] if first else [(3, VR, 256), (N_DEV, 128)]
    return pl.pallas_call(
        functools.partial(settle_body, first=first),
        out_shape=tuple(jax.ShapeDtypeStruct(x, F32) for x in shapes),
        in_specs=[SM, SM] + [VM] * (7 + len(wall)),
        out_specs=(VM,) * len(shapes),
        scratch_shapes=[
            pltpu.VMEM((192, 512), BF),
            pltpu.VMEM((192, 88), BF),
            pltpu.VMEM((88, 128), F32),
            pltpu.VMEM((1, 128), F32),
        ],
        compiler_params=params(),
    )(at, live, p, q, mass, v, conn, coef, stiff, *wall)


def rows_in(at_ref):
    x = lax.broadcasted_iota(jnp.int32, (16, 128), 0) + at_ref[0] * 8 - 3
    return ((x >= 0) & (x < N_GX * 8)).astype(F32)


def wall_step(p, gain, force, inside, depth):
    lane = lax.broadcasted_iota(jnp.int32, (16, 128), 1)
    out = []
    for z in range(depth):
        c = p[z]
        n = pltpu.roll(c, 1, 0) + pltpu.roll(c, 15, 0)
        n = n + jnp.where(lane == 0, 0.0, pltpu.roll(c, 1, 1))
        n = n + jnp.where(lane == 127, 0.0, pltpu.roll(c, 127, 1))
        n = n + p[z + 1]
        if z > 0:
            n = n + p[z - 1]
        out.append(((1.0 - pseudo_weight) * c + gain[z] * (force[z] + n)) * inside)
    return out


def wall_front(at_ref, slab_ref):
    inside = rows_in(at_ref)
    fs = [slab_ref[z * 16 : z * 16 + 16, :] for z in range(4)]
    gain = [pseudo_weight / (6.0 + slab_ref[64 + z * 16 : 64 + z * 16 + 16, :]) for z in range(4)]
    p1 = [gain[z] * fs[z] * inside for z in range(4)]
    p2 = wall_step(p1, gain, fs, inside, 3)
    return inside, fs, gain, p2


def push(wall16, load_ref, seg_ref, f_ref):
    wall = pltpu.roll(wall16, 13, 0)[0:8]
    hi, lo = split(wall)
    table = jnp.concatenate([hi, lo], axis=0)
    i128 = lax.broadcasted_iota(jnp.int32, (128, 256), 0)
    i8 = lax.broadcasted_iota(jnp.int32, (8, 256), 0)
    f_ref[...] = load_ref[...]
    for g in range(4):
        total = jnp.zeros((8, 256), F32)
        for k in range(4):
            face = seg_ref[g, k : k + 1, :].astype(jnp.int32)
            oh = (i128 == ((face >> 8) * 32 + (face & 31))).astype(F32).astype(BF)
            r = jnp.dot(table, oh, preferred_element_type=F32)
            w = jnp.where(i8 == ((face >> 5) & 7), seg_ref[g, 4 + k : 5 + k, :], 0.0)
            total = total + (r[:8] + r[8:]) * w
        traction = total.sum(axis=0, keepdims=True)
        for c in range(3):
            f_ref[c, 12 * g : 12 * g + 1, :] = (
                f_ref[c, 12 * g : 12 * g + 1, :]
                + traction_scale * traction * seg_ref[g, 8 + c : 9 + c, :]
            )


def first_body(at_ref, slab_ref, load_ref, seg_ref, f_ref):
    inside, fs, gain, p2 = wall_front(at_ref, slab_ref)
    push(p2[0], load_ref, seg_ref, f_ref)


def first_force(at, slab, load, seg):
    return pl.pallas_call(
        first_body,
        out_shape=jax.ShapeDtypeStruct((3, VR, 256), F32),
        in_specs=[SM, VM, VM, VM],
        out_specs=VM,
        compiler_params=params(),
    )(at, slab, load, seg)


def weights_of(sums, stiff_ref):
    lane = lax.broadcasted_iota(jnp.int32, (1, 128), 1)
    a, b, c, d = [jnp.where(lane == i, sums, 0.0).sum(axis=1, keepdims=True) for i in range(4)]
    inv = scale_of(stiff_ref)
    alpha = a / b
    beta = (c - b * (b / a)) / (d - c * (c / b))
    return (alpha + beta * (alpha * (c / b))) * inv, -(alpha * beta) * inv


def second_body(at_ref, got_ref, stiff_ref, ws_ref, slab_ref, load_ref, seg_ref, f_ref, wall_ref, sums_ref):
    inside, fs, gain, p2 = wall_front(at_ref, slab_ref)
    sums = got_ref[pl.ds(0, N_DEV, 4), :].sum(axis=0, keepdims=True)
    sums_ref[...] = jnp.broadcast_to(sums, (8, 128))
    c0, c1 = weights_of(sums, stiff_ref)
    gx = at_ref[0]
    wall_ref[...] = jnp.zeros_like(wall_ref)
    wall_ref[3:11, :] = c0 * ws_ref[0:8, :] + c1 * ws_ref[8:16, :]
    for row, by, edge in ((2, -1, 0), (11, 1, N_GX - 1)):
        peer = jnp.clip(gx + by, 0, N_GX - 1) * 4 + at_ref[1]
        got = c0 * got_ref[pl.ds(peer * 4 + 1, 1), :] + c1 * got_ref[pl.ds(peer * 4 + 2, 1), :]
        wall_ref[row : row + 1, :] = jnp.where(jnp.full((1, 128), gx, jnp.int32) == edge, 0.0, got)
    force = [fs[0] + wall_ref[...], fs[1]]
    p3 = wall_step(p2, gain, force, inside, 2)
    p4 = wall_step(p3, gain, force, inside, 1)
    push(p4[0], load_ref, seg_ref, f_ref)


def second_force(at, got, stiff, ws, slab, load, seg):
    return pl.pallas_call(
        second_body,
        out_shape=(
            jax.ShapeDtypeStruct((3, VR, 256), F32),
            jax.ShapeDtypeStruct((16, 128), F32),
            jax.ShapeDtypeStruct((8, 128), F32),
        ),
        in_specs=[SM] + [VM] * 6,
        out_specs=(VM, VM, VM),
        compiler_params=params(),
    )(at, got, stiff, ws, slab, load, seg)


def fluid_body(at_ref, fs_ref, fd_ref, xa_ref, xb_ref, sib_ref, mid_ref, ws_ref, out_ref, src, gain, pa, pb):
    odd = jnp.full((4, 512), at_ref[1] & 1, jnp.int32) == 1
    even = jnp.full((32, 512), at_ref[0] & 1, jnp.int32) == 0
    zero = jnp.zeros((4, 512), F32)
    for j, (ref, dst) in enumerate(((fs_ref, src), (fd_ref, gain))):
        for x in range(14):
            if x < 3:
                own = jnp.where(even, xb_ref[j, x], xa_ref[j, x])
            elif x < 11:
                own = ref[x - 3]
            else:
                own = jnp.where(even, xa_ref[j, x - 11], xb_ref[j, x - 11])
            dst[x, 8:40, :] = own
            sib, mid = sib_ref[j, x], mid_ref[j, x]
            dst[x, 0:8, :] = jnp.concatenate([zero, jnp.where(odd, sib, mid)], axis=0)
            dst[x, 40:48, :] = jnp.concatenate([jnp.where(odd, mid, sib), zero], axis=0)
    lane = lax.broadcasted_iota(jnp.int32, (48, 512), 1)
    y = lax.broadcasted_iota(jnp.int32, (48, 512), 0) + at_ref[1] * 32 - 8
    y_in = ((y >= 0) & (y < 128)).astype(F32)

    def x_in(x):
        gx = at_ref[0] * 8 + x - 3
        return jnp.where((gx >= 0) & (gx < N_GX * 8), 1.0, 0.0).astype(F32)

    def start(x, carry):
        g = pseudo_weight / (6.0 + gain[x]) * (y_in * x_in(x))
        gain[x] = g
        pa[x] = g * src[x]
        return carry

    lax.fori_loop(0, 14, start, 0)

    def new_row(p, x):
        c = p[x]
        n = p[x - 1] + p[x + 1] + pltpu.roll(c, 1, 0) + pltpu.roll(c, 47, 0)
        n = n + jnp.where(lane == 0, 0.0, pltpu.roll(c, 1, 1))
        n = n + jnp.where(lane == 511, 0.0, pltpu.roll(c, 511, 1))
        return (1.0 - pseudo_weight) * c + gain[x] * (src[x] + n)

    def second(x, carry):
        pb[x] = new_row(pa, x)
        return carry

    lax.fori_loop(1, 13, second, 0)

    def add_source(x, carry):
        src[x, :, 0:128] = src[x, :, 0:128] + ws_ref[x]
        return carry

    lax.fori_loop(2, 12, add_source, 0)

    def third(x, carry):
        pa[x] = new_row(pb, x)
        return carry

    lax.fori_loop(2, 12, third, 0)

    def fourth(x, carry):
        out_ref[x - 3] = new_row(pa, x)[8:40]
        return carry

    lax.fori_loop(3, 11, fourth, 0)


def fluid(at, fs, fd, xa, xb, sib, mid, ws):
    return pl.pallas_call(
        fluid_body,
        out_shape=jax.ShapeDtypeStruct((8, 32, 512), F32),
        in_specs=[SM] + [VM] * 7,
        out_specs=VM,
        scratch_shapes=[pltpu.VMEM((14, 48, 512), F32)] * 4,
        compiler_params=params(),
    )(at, fs, fd, xa, xb, sib, mid, ws)


def last_body(s1_ref, got_ref, stiff_ref, f1_ref, w1_ref, f2_ref, w2_ref, out_ref):
    c0, c1 = weights_of(s1_ref[0:1, :], stiff_ref)
    d0, d1 = weights_of(got_ref[...].sum(axis=0, keepdims=True), stiff_ref)
    for c in range(3):
        before = relax_weight * (c0 * f1_ref[c] + c1 * w1_ref[c])
        solved = d0 * f2_ref[c] + d1 * w2_ref[c]
        out_ref[c] = before + relax_weight * (solved - before)


def last(s1, got, stiff, f1, w1, f2, w2):
    return pl.pallas_call(
        last_body,
        out_shape=jax.ShapeDtypeStruct((3, 12, 256), F32),
        in_specs=[VM] * 7,
        out_specs=VM,
        compiler_params=params(),
    )(s1, got, stiff, f1, w1, f2, w2)


def local(
    fluid_source,
    fluid_diag,
    stiff_ref,
    elem_coef,
    connect,
    live_count,
    node_mass,
    solid_load,
    wet_normal,
    trac_face,
    trac_weight,
    wall_node,
    wall_weight,
):
    gx = lax.axis_index("gx")
    gy = lax.axis_index("gy")
    core = gy & 1
    yhi = gy >> 1
    at = jnp.stack([gx, gy]).astype(jnp.int32)

    def in_order(bit, own, other):
        return jnp.concatenate([jnp.where(bit == 0, own, other), jnp.where(bit == 0, other, own)], axis=0)

    even = gx % 2 == 0

    def beside(to_low, to_high):
        first = [(i, i ^ 1) for i in range(N_GX)]
        second = [(i, i + 1) for i in range(1, N_GX - 1, 2)] + [(i + 1, i) for i in range(1, N_GX - 1, 2)]
        a = lax.ppermute(jnp.where(even, to_high, to_low), "gx", first)
        b = lax.ppermute(jnp.where(even, to_low, to_high), "gx", second)
        return a, b

    both = jnp.stack([fluid_source, fluid_diag])
    xa, xb = beside(both[:, 0:3], both[:, 5:8])

    own = pack_parts(
        stiff_ref, solid_load, node_mass.reshape(1, 3072), trac_face, trac_weight, wet_normal
    )
    wide = pack_wall(at, fluid_source, fluid_diag, xa, xb, wall_node, wall_weight)
    near = swap(jnp.concatenate([own, wide], axis=0), CORE)
    pair = jnp.concatenate([in_order(core, own, near[:128]), wide + near[128:]], axis=0)
    far = swap(pair, YHI)
    wide = pair[256:] + far[256:]
    slab, pick = wide[:128], wide[128:]
    parts = in_order(yhi, pair[:256], far[:256]).reshape(4, 2, 64, 128)
    parts = jnp.concatenate([parts[:, 0], parts[:, 1]], axis=2)
    seg = parts[:, 48:64]
    load = parts[:, :36].reshape(4, 3, 12, 256).transpose(1, 0, 2, 3).reshape(3, OWN, 256)
    load = jnp.pad(load, ((0, 0), (0, VR - OWN), (0, 0)))
    mass = jnp.pad(parts[:, 36:48].reshape(OWN, 256), ((0, VR - OWN), (0, 0)))
    coef = elem_coef.reshape(1, 384)
    row = lax.broadcasted_iota(jnp.int32, (3, VR, 256), 1)

    def to_all(x):
        return lax.all_to_all(x, AXES, 0, 0, tiled=True)

    def pair_sum(v):
        s = stiff_apply(live_count, v, connect, coef, stiff_ref)
        a, b = beside(s[:, 0, :], s[:, OWN, :])
        below, above = jnp.where(even, b, a), jnp.where(even, a, b)
        s = s + jnp.where(row == 0, below[:, None, :], 0.0) + jnp.where(row == OWN, above[:, None, :], 0.0)
        return s + swap(s, CORE)

    f1 = first_force(at, slab, load, seg)
    following = from_gx(jnp.concatenate([f1[:, 0, :], mass[0:1]], axis=0), -1)
    f1 = jnp.where(row == OWN, following[0:3, None, :], f1)
    mass = jnp.where(row[0] == OWN, following[3:4], mass)
    pair1 = pair_sum(f1)

    xlo, xhi = jnp.where(even, xb, xa), jnp.where(even, xa, xb)
    low = jnp.concatenate([xlo[:, :, 0:4], both[:, :, 0:4], xhi[:, :, 0:4]], axis=1)
    high = jnp.concatenate([xlo[:, :, 28:32], both[:, :, 28:32], xhi[:, :, 28:32]], axis=1)
    sides = (jnp.where(core == 0, high, low), jnp.where(core == 0, low, high))
    sides, pair1 = lax.optimization_barrier((sides, pair1))
    other1 = swap(pair1, YHI)
    sib = swap(sides[0], CORE)
    mid = lax.ppermute(sides[1], "gy", [(1, 2), (2, 1)])
    pair1, sib, mid = lax.optimization_barrier((pair1, sib, mid))
    w1, out1, wsb = settle(at, live_count, pair1, other1, mass, f1, connect, coef, stiff_ref, (seg, pick))
    f2, ws, s1 = second_force(at, to_all(out1), stiff_ref, wsb, slab, load, seg)
    following = from_gx(f2[:, 0, :], -1)
    f2 = jnp.where(row == OWN, following[:, None, :], f2)
    pair2 = pair_sum(f2)

    padded = jnp.pad(ws, ((0, 0), (8, 8)))
    wall = lax.dynamic_slice_in_dim(padded, gy * 32, 48, axis=1)
    lane = lax.broadcasted_iota(jnp.int32, (16, 48, 128), 2)
    wall = jnp.where(lane == 0, wall[:, :, None], 0.0)
    wall, pair2 = lax.optimization_barrier((wall, pair2))
    other2 = swap(pair2, YHI)
    pressure = fluid(at, fluid_source, fluid_diag, xa, xb, sib, mid, wall)
    pair2, pressure = lax.optimization_barrier((pair2, pressure))
    w2, out2 = settle(at, live_count, pair2, other2, mass, f2, connect, coef, stiff_ref)

    def mine(x):
        return lax.dynamic_slice_in_dim(x, gy * 12, 12, axis=1)

    displacement = last(s1, to_all(out2), stiff_ref, mine(f1), mine(w1), mine(f2), mine(w2)).reshape(3, 3072)
    return pressure, displacement


def solution(mesh):
    in_specs = (
        P("gx", "gy", None),
        P("gx", "gy", None),
        P(),
        P(("gx", "gy")),
        P(None, ("gx", "gy")),
        P(("gx", "gy")),
        P(("gx", "gy")),
        P(None, ("gx", "gy")),
        P(None, ("gx", "gy")),
        P(None, ("gx", "gy")),
        P(None, ("gx", "gy")),
        P(None, "gx", "gy"),
        P(None, "gx", "gy"),
    )
    out_specs = (P("gx", "gy", None), P(None, ("gx", "gy")))
    return jax.shard_map(local, mesh=mesh, in_specs=in_specs, out_specs=out_specs, check_vma=False)
```

```python
import functools

import jax
import jax.numpy as jnp
from jax import lax
from jax.experimental import pallas as pl
from jax.experimental.pallas import tpu as pltpu
from jax.sharding import PartitionSpec as P

F32 = jnp.float32
BF = jnp.bfloat16
AXES = ("gx", "gy")
N_GX = 32
N_DEV = 128
LR = 64
VR = 56
OWN = 48
CORE = 1
YHI = 2

pseudo_weight = 0.8
traction_scale = 30.0
motion_scale = 2.0
relax_weight = 0.5

VM = pl.BlockSpec(memory_space=pltpu.VMEM)
SM = pl.BlockSpec(memory_space=pltpu.SMEM)


def params(mib=40):
    return pltpu.CompilerParams(vmem_limit_bytes=mib << 20)


def swap(x, mask):
    return lax.ppermute(x, AXES, [(i, i ^ mask) for i in range(N_DEV)])


def from_gx(x, by):
    return lax.ppermute(x, "gx", [(i, i + by) for i in range(N_GX) if 0 <= i + by < N_GX])


def from_gy(x, by):
    return lax.ppermute(x, "gy", [(i, i + by) for i in range(4) if 0 <= i + by < 4])


def split(v):
    hi = v.astype(BF)
    return hi, (v - hi.astype(F32)).astype(BF)


def scale_of(stiff_ref):
    r = lax.broadcasted_iota(jnp.int32, (81, 81), 0)
    c = lax.broadcasted_iota(jnp.int32, (81, 81), 1)
    diag = jnp.where(r == c, stiff_ref[...], 0.0)
    trace = diag.sum(axis=1, keepdims=True).sum(axis=0, keepdims=True)
    return 1.0 / jnp.maximum(1.0, trace)


def fill_stiff(stiff_ref, s_scr):
    s_scr[...] = jnp.zeros_like(s_scr)
    hi, lo = split(jnp.pad(stiff_ref[...] * scale_of(stiff_ref), ((0, 15), (0, 7))))
    s_scr[0:96, :] = hi
    s_scr[96:192, :] = lo


def fill_table(v_ref, t_scr):
    for c in range(3):
        v = jnp.concatenate([v_ref[c], jnp.zeros((LR - VR, 256), F32)], axis=0)
        hi, lo = split(v)
        t_scr[c * LR : (c + 1) * LR, 0:256] = hi
        t_scr[c * LR : (c + 1) * LR, 256:512] = lo


def block_of(b):
    return pl.ds(pl.multiple_of(b * 128, 128), 128)


def forces_of(x, s_scr, coef_ref, live, b):
    xh, xl = split(x)
    r = jnp.dot(s_scr[...], xh, preferred_element_type=F32)
    prod = r[:88] + r[96:184] + jnp.dot(s_scr[0:96, :], xl, preferred_element_type=F32)[:88]
    slot = lax.broadcasted_iota(jnp.int32, (1, 128), 1) + b * 128
    return prod * jnp.where(slot < live, coef_ref[:, block_of(b)], 0.0)


def apply_body(live_ref, v_ref, conn_ref, coef_ref, stiff_ref, out_ref, t_scr, s_scr, oh_scr, ml_scr, x_scr, a_scr, acc):
    fill_table(v_ref, t_scr)
    fill_stiff(stiff_ref, s_scr)
    x_scr[80:88, :] = jnp.zeros((8, 128), F32)
    acc[...] = jnp.zeros_like(acc)
    i256 = lax.broadcasted_iota(jnp.int32, (256, 128), 0)
    i64 = lax.broadcasted_iota(jnp.int32, (LR, 128), 0)
    oh_scr[:, 27 * 128 :] = jnp.zeros((256, 128), BF)
    ml_scr[:, 27 * 128 :] = jnp.zeros((LR, 128), BF)
    a_scr[:, 27 * 128 :] = jnp.zeros((384, 128), BF)
    live = live_ref[0]

    def block(b, carry):
        for p in range(14):
            for h in range(2):
                k = 2 * p + h
                if k < 27:
                    sl = slice(k * 128, k * 128 + 128)
                    idx = conn_ref[k : k + 1, block_of(b)]
                    oh_scr[:, sl] = (i256 == (idx & 255)).astype(F32).astype(BF)
                    ml_scr[:, sl] = (i64 == (idx >> 8)).astype(F32).astype(BF)
            sp = slice(p * 256, p * 256 + 256)
            oh = oh_scr[:, sp]
            g = jnp.dot(t_scr[...], jnp.concatenate([oh, oh], axis=0), preferred_element_type=F32)
            m = ml_scr[:, sp].astype(F32)
            for c in range(3):
                s = (g[c * LR : (c + 1) * LR] * m).sum(axis=0, keepdims=True)
                for h in range(2):
                    k = 2 * p + h
                    if k < 27:
                        x_scr[c * 27 + k : c * 27 + k + 1, :] = s[:, h * 128 : h * 128 + 128]
        prod = forces_of(x_scr[...], s_scr, coef_ref, live, b)
        ph = prod.astype(BF).astype(F32)
        parts = (ph, prod - ph)
        for k in range(27):
            sl = slice(k * 128, k * 128 + 128)
            m = ml_scr[:, sl].reshape(4, 16, 128)
            for c in range(3):
                row = c * 27 + k
                for j, src in enumerate(parts):
                    r16 = jnp.broadcast_to(src[row : row + 1, :], (16, 128)).astype(BF)
                    at = j * 192 + c * LR
                    a_scr[at : at + LR, sl] = (m * r16[None]).reshape(LR, 128)
        acc[...] += lax.dot_general(
            a_scr[...], oh_scr[...], (((1,), (1,)), ((), ())), preferred_element_type=F32
        )
        return carry

    lax.fori_loop(0, (live + 127) // 128, block, 0)
    for c in range(3):
        s = acc[c * LR : (c + 1) * LR, :] + acc[192 + c * LR : 192 + (c + 1) * LR, :]
        out_ref[c] = s[:VR]


def stiff_apply(live, v, conn, coef, stiff):
    return pl.pallas_call(
        apply_body,
        out_shape=jax.ShapeDtypeStruct((3, VR, 256), F32),
        in_specs=[SM] + [VM] * 4,
        out_specs=VM,
        scratch_shapes=[
            pltpu.VMEM((192, 512), BF),
            pltpu.VMEM((192, 88), BF),
            pltpu.VMEM((256, 3584), BF),
            pltpu.VMEM((LR, 3584), BF),
            pltpu.VMEM((88, 128), F32),
            pltpu.VMEM((384, 3584), BF),
            pltpu.VMEM((384, 256), F32),
        ],
        compiler_params=params(),
        cost_estimate=pl.CostEstimate(flops=6 * 10**9, bytes_accessed=24 * 10**6, transcendentals=0),
    )(live, v, conn, coef, stiff)


def pack_parts_body(stiff_ref, load_ref, mass_ref, face_ref, tw_ref, normal_ref, out_ref):
    def put(at, row):
        out_ref[at : at + 1, :] = row[:, :128]
        out_ref[64 + at : 65 + at, :] = row[:, 128:]

    scale = scale_of(stiff_ref)
    for r in range(12):
        sl = slice(r * 256, r * 256 + 256)
        for c in range(3):
            put(c * 12 + r, load_ref[c : c + 1, sl])
        put(36 + r, mass_ref[:, sl] * scale)
    for k in range(4):
        put(48 + k, face_ref[k : k + 1, :].astype(F32))
        put(52 + k, tw_ref[k : k + 1, :])
    for c in range(3):
        put(56 + c, normal_ref[c : c + 1, :])
    zero = jnp.zeros((1, 256), F32)
    for r in range(59, 64):
        put(r, zero)


def pack_parts(stiff, load, mass, face, weight, normal):
    return pl.pallas_call(
        pack_parts_body,
        out_shape=jax.ShapeDtypeStruct((128, 128), F32),
        in_specs=[VM] * 6,
        out_specs=VM,
        compiler_params=params(),
    )(stiff, load, mass, face, weight, normal)


def pack_wall_body(at_ref, fs_ref, fd_ref, xa_ref, xb_ref, node_ref, ww_ref, out_ref):
    out_ref[...] = jnp.zeros_like(out_ref)
    even = jnp.full((32, 128), at_ref[0] & 1, jnp.int32) == 0
    for j, ref in enumerate((fs_ref, fd_ref)):
        for x in range(14):
            if x < 3:
                v = jnp.where(even, xb_ref[j, x], xa_ref[j, x])
            elif x < 11:
                v = ref[x - 3]
            else:
                v = jnp.where(even, xa_ref[j, x - 11], xb_ref[j, x - 11])
            t = v.T
            for z in range(4):
                at = j * 64 + z * 16 + x
                out_ref[at : at + 1, 0:32] = t[z : z + 1, :]
    for k in range(4):
        out_ref[128 + k * 8 : 136 + k * 8, 0:32] = node_ref[k].astype(F32)
        out_ref[160 + k * 8 : 168 + k * 8, 0:32] = ww_ref[k]
    out_ref[...] = pltpu.roll(out_ref[...], at_ref[1] * 32, 1)


def pack_wall(at, fs, fd, xa, xb, node, weight):
    def block(*shape):
        return pl.BlockSpec(shape, lambda i: (0,) * len(shape))

    return pl.pallas_call(
        pack_wall_body,
        grid=(1,),
        out_shape=jax.ShapeDtypeStruct((192, 128), F32),
        in_specs=[
            SM,
            block(8, 32, 128),
            block(8, 32, 128),
            block(2, 3, 32, 128),
            block(2, 3, 32, 128),
            block(4, 8, 32),
            block(4, 8, 32),
        ],
        out_specs=block(192, 128),
        compiler_params=params(),
    )(at, fs, fd, xa, xb, node, weight)


def source_of(vec_ref, seg_ref, pick_ref):
    rows = []
    for g in range(4):
        total = jnp.zeros((1, 256), F32)
        for c in range(3):
            total = total + seg_ref[g, 8 + c : 9 + c, :] * vec_ref[c, 12 * g : 12 * g + 1, :]
        rows.append(total)
    return split(jnp.concatenate(rows + [jnp.zeros((4, 256), F32)], axis=0))


def settle_body(*refs, first):
    at_ref, live_ref, p_ref, q_ref, edge_ref, mass_ref, v_ref, conn_ref, coef_ref, stiff_ref = refs[:10]
    if first:
        seg_ref, pick_ref, w_ref, out_ref, ws_ref = refs[10:15]
    else:
        w_ref, out_ref = refs[10:12]
    t_scr, s_scr, x_scr, acc = refs[-4:]
    keep = lax.broadcasted_iota(jnp.int32, (VR, 256), 0)
    end = jnp.where(at_ref[0] == N_GX - 1, OWN, OWN + 1)
    mask = (keep < end).astype(F32)
    mass = mass_ref[...]
    dots = [jnp.zeros((8, 256), F32) for _ in range(4)]
    for c in range(3):
        v = v_ref[c]
        w = p_ref[c] + q_ref[c]
        w = w + jnp.where(keep == 0, edge_ref[0, c : c + 1, :], jnp.where(keep == OWN, edge_ref[1, c : c + 1, :], 0.0))
        w = (w + mass * v) * mask
        w_ref[c] = w
        for i, (x, y) in enumerate(((v, v), (v, w), (w, w), (w, mass * w))):
            dots[i] = dots[i] + (x[:OWN] * y[:OWN]).reshape(6, 8, 256).sum(axis=0)
    dots = [0.25 * d.sum(axis=0, keepdims=True).sum(axis=1, keepdims=True) for d in dots]

    if first:
        hf, lf = source_of(v_ref, seg_ref, pick_ref)
        hw, lw = source_of(w_ref, seg_ref, pick_ref)
        table = jnp.concatenate([hf, lf, hw, lw], axis=0)
        n256 = lax.broadcasted_iota(jnp.int32, (256, 128), 0)
        n8 = lax.broadcasted_iota(jnp.int32, (8, 128), 0)
        for x in range(8):
            tf = jnp.zeros((8, 128), F32)
            tw = jnp.zeros((8, 128), F32)
            for k in range(4):
                row = k * 8 + x
                node = pick_ref[row : row + 1, :].astype(jnp.int32)
                oh = (n256 == (node & 255)).astype(F32).astype(BF)
                r = jnp.dot(table, oh, preferred_element_type=F32)
                u = jnp.where(n8 == (node >> 8), pick_ref[32 + row : 33 + row, :], 0.0)
                tf = tf + (r[0:8] + r[8:16]) * u
                tw = tw + (r[16:24] + r[24:32]) * u
            ws_ref[x : x + 1, :] = (motion_scale * relax_weight) * tf.sum(axis=0, keepdims=True)
            ws_ref[8 + x : 9 + x, :] = (motion_scale * relax_weight) * tw.sum(axis=0, keepdims=True)

    fill_table(w_ref, t_scr)
    fill_stiff(stiff_ref, s_scr)
    acc[...] = jnp.zeros_like(acc)
    x_scr[80:88, :] = jnp.zeros((8, 128), F32)
    i256 = lax.broadcasted_iota(jnp.int32, (256, 128), 0)
    i64 = lax.broadcasted_iota(jnp.int32, (LR, 128), 0)
    live = live_ref[0]

    def block(b, carry):
        for p in range(14):
            pieces, masks = [], []
            for k in (2 * p, 2 * p + 1):
                idx = conn_ref[min(k, 26) : min(k, 26) + 1, block_of(b)]
                pieces.append((i256 == (idx & 255)).astype(F32).astype(BF))
                masks.append((i64 == (idx >> 8)).astype(F32))
            oh = jnp.concatenate(pieces, axis=1)
            g = jnp.dot(t_scr[...], jnp.concatenate([oh, oh], axis=0), preferred_element_type=F32)
            m = jnp.concatenate(masks, axis=1)
            for c in range(3):
                s = (g[c * LR : (c + 1) * LR] * m).sum(axis=0, keepdims=True)
                for h in range(2):
                    k = 2 * p + h
                    if k < 27:
                        x_scr[c * 27 + k : c * 27 + k + 1, :] = s[:, h * 128 : h * 128 + 128]
        x = x_scr[...]
        acc[...] += (forces_of(x, s_scr, coef_ref, live, b) * x).sum(axis=0, keepdims=True)
        return carry

    lax.fori_loop(0, (live + 127) // 128, block, 0)
    dots[3] = dots[3] + acc[...].sum(axis=1, keepdims=True)
    lane = lax.broadcasted_iota(jnp.int32, (1, 128), 1)
    row = jnp.zeros((1, 128), F32)
    for i in range(4):
        row = jnp.where(lane == i, dots[i], row)
    row = jnp.broadcast_to(row, (N_DEV, 128))
    if first:
        peer = lax.broadcasted_iota(jnp.int32, (N_DEV, 128), 0) >> 2
        after = peer > at_ref[0]
        out_ref[pl.ds(0, N_DEV, 4), :] = row
        out_ref[pl.ds(1, N_DEV, 4), :] = jnp.where(after, ws_ref[7:8, :], ws_ref[0:1, :])
        out_ref[pl.ds(2, N_DEV, 4), :] = jnp.where(after, ws_ref[15:16, :], ws_ref[8:9, :])
        out_ref[pl.ds(3, N_DEV, 4), :] = jnp.zeros((N_DEV, 128), F32)
    else:
        out_ref[...] = row


def settle(at, live, p, q, edge, mass, v, conn, coef, stiff, wall=()):
    first = bool(wall)
    shapes = [(3, VR, 256), (4 * N_DEV, 128), (16, 128)] if first else [(3, VR, 256), (N_DEV, 128)]
    return pl.pallas_call(
        functools.partial(settle_body, first=first),
        out_shape=tuple(jax.ShapeDtypeStruct(x, F32) for x in shapes),
        in_specs=[SM, SM] + [VM] * (8 + len(wall)),
        out_specs=(VM,) * len(shapes),
        scratch_shapes=[
            pltpu.VMEM((192, 512), BF),
            pltpu.VMEM((192, 88), BF),
            pltpu.VMEM((88, 128), F32),
            pltpu.VMEM((1, 128), F32),
        ],
        compiler_params=params(),
        cost_estimate=pl.CostEstimate(flops=6 * 10**9, bytes_accessed=24 * 10**6, transcendentals=0),
    )(at, live, p, q, edge, mass, v, conn, coef, stiff, *wall)


def rows_in(at_ref):
    x = lax.broadcasted_iota(jnp.int32, (16, 128), 0) + at_ref[0] * 8 - 3
    return ((x >= 0) & (x < N_GX * 8)).astype(F32)


def wall_step(p, gain, force, inside, depth):
    lane = lax.broadcasted_iota(jnp.int32, (16, 128), 1)
    out = []
    for z in range(depth):
        c = p[z]
        n = pltpu.roll(c, 1, 0) + pltpu.roll(c, 15, 0)
        n = n + jnp.where(lane == 0, 0.0, pltpu.roll(c, 1, 1))
        n = n + jnp.where(lane == 127, 0.0, pltpu.roll(c, 127, 1))
        n = n + p[z + 1]
        if z > 0:
            n = n + p[z - 1]
        out.append(((1.0 - pseudo_weight) * c + gain[z] * (force[z] + n)) * inside)
    return out


def wall_front(at_ref, slab_ref):
    inside = rows_in(at_ref)
    fs = [slab_ref[z * 16 : z * 16 + 16, :] for z in range(4)]
    gain = [pseudo_weight / (6.0 + slab_ref[64 + z * 16 : 64 + z * 16 + 16, :]) for z in range(4)]
    p1 = [gain[z] * fs[z] * inside for z in range(4)]
    p2 = wall_step(p1, gain, fs, inside, 3)
    return inside, fs, gain, p2


def push(wall16, load_ref, seg_ref, f_ref):
    wall = pltpu.roll(wall16, 13, 0)[0:8]
    hi, lo = split(wall)
    table = jnp.concatenate([hi, lo], axis=0)
    i128 = lax.broadcasted_iota(jnp.int32, (128, 256), 0)
    i8 = lax.broadcasted_iota(jnp.int32, (8, 256), 0)
    f_ref[...] = load_ref[...]
    for g in range(4):
        total = jnp.zeros((8, 256), F32)
        for k in range(4):
            face = seg_ref[g, k : k + 1, :].astype(jnp.int32)
            oh = (i128 == ((face >> 8) * 32 + (face & 31))).astype(F32).astype(BF)
            r = jnp.dot(table, oh, preferred_element_type=F32)
            w = jnp.where(i8 == ((face >> 5) & 7), seg_ref[g, 4 + k : 5 + k, :], 0.0)
            total = total + (r[:8] + r[8:]) * w
        traction = total.sum(axis=0, keepdims=True)
        for c in range(3):
            f_ref[c, 12 * g : 12 * g + 1, :] = (
                f_ref[c, 12 * g : 12 * g + 1, :]
                + traction_scale * traction * seg_ref[g, 8 + c : 9 + c, :]
            )


def first_body(at_ref, slab_ref, load_ref, seg_ref, f_ref):
    inside, fs, gain, p2 = wall_front(at_ref, slab_ref)
    push(p2[0], load_ref, seg_ref, f_ref)


def first_force(at, slab, load, seg):
    return pl.pallas_call(
        first_body,
        out_shape=jax.ShapeDtypeStruct((3, VR, 256), F32),
        in_specs=[SM, VM, VM, VM],
        out_specs=VM,
        compiler_params=params(),
    )(at, slab, load, seg)


def weights_of(sums, stiff_ref):
    lane = lax.broadcasted_iota(jnp.int32, (1, 128), 1)
    a, b, c, d = [jnp.where(lane == i, sums, 0.0).sum(axis=1, keepdims=True) for i in range(4)]
    inv = scale_of(stiff_ref)
    alpha = a / b
    beta = (c - b * (b / a)) / (d - c * (c / b))
    return (alpha + beta * (alpha * (c / b))) * inv, -(alpha * beta) * inv


def second_body(at_ref, got_ref, stiff_ref, ws_ref, slab_ref, load_ref, seg_ref, f_ref, wall_ref, sums_ref):
    inside, fs, gain, p2 = wall_front(at_ref, slab_ref)
    sums = got_ref[pl.ds(0, N_DEV, 4), :].sum(axis=0, keepdims=True)
    sums_ref[...] = jnp.broadcast_to(sums, (8, 128))
    c0, c1 = weights_of(sums, stiff_ref)
    gx = at_ref[0]
    wall_ref[...] = jnp.zeros_like(wall_ref)
    wall_ref[3:11, :] = c0 * ws_ref[0:8, :] + c1 * ws_ref[8:16, :]
    for row, by, edge in ((2, -1, 0), (11, 1, N_GX - 1)):
        peer = jnp.clip(gx + by, 0, N_GX - 1) * 4 + at_ref[1]
        got = c0 * got_ref[pl.ds(peer * 4 + 1, 1), :] + c1 * got_ref[pl.ds(peer * 4 + 2, 1), :]
        wall_ref[row : row + 1, :] = jnp.where(jnp.full((1, 128), gx, jnp.int32) == edge, 0.0, got)
    force = [fs[0] + wall_ref[...], fs[1]]
    p3 = wall_step(p2, gain, force, inside, 2)
    p4 = wall_step(p3, gain, force, inside, 1)
    push(p4[0], load_ref, seg_ref, f_ref)


def second_force(at, got, stiff, ws, slab, load, seg):
    return pl.pallas_call(
        second_body,
        out_shape=(
            jax.ShapeDtypeStruct((3, VR, 256), F32),
            jax.ShapeDtypeStruct((16, 128), F32),
            jax.ShapeDtypeStruct((8, 128), F32),
        ),
        in_specs=[SM] + [VM] * 6,
        out_specs=(VM, VM, VM),
        compiler_params=params(),
    )(at, got, stiff, ws, slab, load, seg)


def fluid_body(at_ref, fs_ref, fd_ref, xa_ref, xb_ref, sib_ref, mid_ref, ws_ref, out_ref, src, gain, pa, pb):
    odd = jnp.full((4, 512), at_ref[1] & 1, jnp.int32) == 1
    even = jnp.full((32, 512), at_ref[0] & 1, jnp.int32) == 0
    zero = jnp.zeros((4, 512), F32)
    for j, (ref, dst) in enumerate(((fs_ref, src), (fd_ref, gain))):
        for x in range(14):
            if x < 3:
                own = jnp.where(even, xb_ref[j, x], xa_ref[j, x])
            elif x < 11:
                own = ref[x - 3]
            else:
                own = jnp.where(even, xa_ref[j, x - 11], xb_ref[j, x - 11])
            dst[x, 8:40, :] = own
            sib, mid = sib_ref[j, x], mid_ref[j, x]
            dst[x, 0:8, :] = jnp.concatenate([zero, jnp.where(odd, sib, mid)], axis=0)
            dst[x, 40:48, :] = jnp.concatenate([jnp.where(odd, mid, sib), zero], axis=0)
    lane = lax.broadcasted_iota(jnp.int32, (48, 512), 1)
    y = lax.broadcasted_iota(jnp.int32, (48, 512), 0) + at_ref[1] * 32 - 8
    y_in = ((y >= 0) & (y < 128)).astype(F32)

    def x_in(x):
        gx = at_ref[0] * 8 + x - 3
        return jnp.where((gx >= 0) & (gx < N_GX * 8), 1.0, 0.0).astype(F32)

    def start(x, carry):
        g = pseudo_weight / (6.0 + gain[x]) * (y_in * x_in(x))
        gain[x] = g
        pa[x] = g * src[x]
        return carry

    lax.fori_loop(0, 14, start, 0)

    def new_row(p, x):
        c = p[x]
        n = p[x - 1] + p[x + 1] + pltpu.roll(c, 1, 0) + pltpu.roll(c, 47, 0)
        n = n + jnp.where(lane == 0, 0.0, pltpu.roll(c, 1, 1))
        n = n + jnp.where(lane == 511, 0.0, pltpu.roll(c, 511, 1))
        return (1.0 - pseudo_weight) * c + gain[x] * (src[x] + n)

    def second(x, carry):
        pb[x] = new_row(pa, x)
        return carry

    lax.fori_loop(1, 13, second, 0)

    def add_source(x, carry):
        src[x, :, 0:128] = src[x, :, 0:128] + ws_ref[x]
        return carry

    lax.fori_loop(2, 12, add_source, 0)

    def third(x, carry):
        pa[x] = new_row(pb, x)
        return carry

    lax.fori_loop(2, 12, third, 0)

    def fourth(x, carry):
        out_ref[x - 3] = new_row(pa, x)[8:40]
        return carry

    lax.fori_loop(3, 11, fourth, 0)


def fluid(at, fs, fd, xa, xb, sib, mid, ws):
    return pl.pallas_call(
        fluid_body,
        out_shape=jax.ShapeDtypeStruct((8, 32, 512), F32),
        in_specs=[SM] + [VM] * 7,
        out_specs=VM,
        scratch_shapes=[pltpu.VMEM((14, 48, 512), F32)] * 4,
        compiler_params=params(),
        cost_estimate=pl.CostEstimate(flops=10**8, bytes_accessed=20 * 10**6, transcendentals=0),
    )(at, fs, fd, xa, xb, sib, mid, ws)


def last_body(s1_ref, got_ref, stiff_ref, f1_ref, w1_ref, f2_ref, w2_ref, out_ref):
    c0, c1 = weights_of(s1_ref[0:1, :], stiff_ref)
    d0, d1 = weights_of(got_ref[...].sum(axis=0, keepdims=True), stiff_ref)
    for c in range(3):
        before = relax_weight * (c0 * f1_ref[c] + c1 * w1_ref[c])
        solved = d0 * f2_ref[c] + d1 * w2_ref[c]
        out_ref[c] = before + relax_weight * (solved - before)


def last(s1, got, stiff, f1, w1, f2, w2):
    return pl.pallas_call(
        last_body,
        out_shape=jax.ShapeDtypeStruct((3, 12, 256), F32),
        in_specs=[VM] * 7,
        out_specs=VM,
        compiler_params=params(),
    )(s1, got, stiff, f1, w1, f2, w2)


def local(
    fluid_source,
    fluid_diag,
    stiff_ref,
    elem_coef,
    connect,
    live_count,
    node_mass,
    solid_load,
    wet_normal,
    trac_face,
    trac_weight,
    wall_node,
    wall_weight,
):
    gx = lax.axis_index("gx")
    gy = lax.axis_index("gy")
    core = gy & 1
    yhi = gy >> 1
    at = jnp.stack([gx, gy]).astype(jnp.int32)

    def in_order(bit, own, other):
        return jnp.concatenate([jnp.where(bit == 0, own, other), jnp.where(bit == 0, other, own)], axis=0)

    even = gx % 2 == 0
    low_pairs = [(i, i ^ 1) for i in range(N_GX)]
    high_pairs = [(i, i + 1) for i in range(1, N_GX - 1, 2)]
    high_pairs = high_pairs + [(j, i) for i, j in high_pairs]

    def beside(to_low, to_high, cross=False):
        sends = jnp.where(even, to_high, to_low), jnp.where(even, to_low, to_high)
        got = []
        for send, pairs in zip(sends, (low_pairs, high_pairs)):
            if cross:
                both_ends = [(4 * i + g, 4 * j + (g ^ (2 * (g & 1)))) for i, j in pairs for g in range(4)]
                got.append(lax.ppermute(send, AXES, both_ends))
            else:
                got.append(lax.ppermute(send, "gx", pairs))
        return got

    def three(part):
        return jnp.stack([fluid_source[part], fluid_diag[part]])

    sa, sb = beside(three(slice(0, 3))[..., :128], three(slice(5, 8))[..., :128])

    own = pack_parts(
        stiff_ref, solid_load, node_mass.reshape(1, 3072), trac_face, trac_weight, wet_normal
    )
    wide = pack_wall(at, fluid_source, fluid_diag, sa, sb, wall_node, wall_weight)
    near = swap(jnp.concatenate([own, wide], axis=0), CORE)
    pair = jnp.concatenate([in_order(core, own, near[:128]), wide + near[128:]], axis=0)
    far = swap(pair, YHI)
    wide = pair[256:] + far[256:]
    slab, pick = wide[:128], wide[128:]
    parts = in_order(yhi, pair[:256], far[:256]).reshape(4, 2, 64, 128)
    parts = jnp.concatenate([parts[:, 0], parts[:, 1]], axis=2)
    seg = parts[:, 48:64]
    load = parts[:, :36].reshape(4, 3, 12, 256).transpose(1, 0, 2, 3).reshape(3, OWN, 256)
    load = jnp.pad(load, ((0, 0), (0, VR - OWN), (0, 0)))
    mass = jnp.pad(parts[:, 36:48].reshape(OWN, 256), ((0, VR - OWN), (0, 0)))
    coef = elem_coef.reshape(1, 384)
    row = lax.broadcasted_iota(jnp.int32, (3, VR, 256), 1)

    def to_all(x):
        return lax.all_to_all(x, AXES, 0, 0, tiled=True)

    def exchange(s):
        pair = s + swap(s, CORE)
        far = swap(pair, YHI)
        ab = beside(pair[:, 0, :], pair[:, OWN, :], cross=True)
        return pair, far, ab

    def edges(far, ab):
        far, (a, b) = lax.optimization_barrier((far, ab))
        got = jnp.stack([jnp.where(even, b, a), jnp.where(even, a, b)])
        return far, got + swap(got, CORE)

    f1 = first_force(at, slab, load, seg)
    following = from_gx(jnp.concatenate([f1[:, 0, :], mass[0:1]], axis=0), -1)
    f1 = jnp.where(row == OWN, following[0:3, None, :], f1)
    mass = jnp.where(row[0] == OWN, following[3:4], mass)

    pair1, far1, ab = exchange(stiff_apply(live_count, f1, connect, coef, stiff_ref))
    far1, edge1 = edges(far1, ab)
    w1, out1, wsb = settle(
        at, live_count, pair1, far1, edge1, mass, f1, connect, coef, stiff_ref, (seg, pick)
    )
    rows, out1 = lax.optimization_barrier(((three(slice(0, 3)), three(slice(5, 8))), out1))
    got1 = to_all(out1)
    xa, xb = beside(*rows)
    f2, ws, s1 = second_force(at, got1, stiff_ref, wsb, slab, load, seg)
    following = from_gx(f2[:, 0, :], -1)
    f2 = jnp.where(row == OWN, following[:, None, :], f2)
    f2, xa, xb = lax.optimization_barrier((f2, xa, xb))
    pair2, far2, ab = exchange(stiff_apply(live_count, f2, connect, coef, stiff_ref))

    xlo, xhi = jnp.where(even, xb, xa), jnp.where(even, xa, xb)

    def columns(part):
        middle = jnp.stack([fluid_source[:, part], fluid_diag[:, part]])
        return jnp.concatenate([xlo[:, :, part], middle, xhi[:, :, part]], axis=1)

    low, high = columns(slice(0, 4)), columns(slice(28, 32))
    sides = (jnp.where(core == 0, high, low), jnp.where(core == 0, low, high))
    padded = jnp.pad(ws, ((0, 0), (8, 8)))
    wall = lax.dynamic_slice_in_dim(padded, gy * 32, 48, axis=1)
    lane = lax.broadcasted_iota(jnp.int32, (16, 48, 128), 2)
    wall = jnp.where(lane == 0, wall[:, :, None], 0.0)
    sides, wall, pair2 = lax.optimization_barrier((sides, wall, pair2))
    far2, edge2 = edges(far2, ab)
    sides, far2, edge2 = lax.optimization_barrier((sides, far2, edge2))
    sib = swap(sides[0], CORE)
    mid = lax.ppermute(sides[1], "gy", [(1, 2), (2, 1)])
    w2, out2 = settle(at, live_count, pair2, far2, edge2, mass, f2, connect, coef, stiff_ref)
    out2, sib, mid = lax.optimization_barrier((out2, sib, mid))
    got2 = to_all(out2)
    pressure = fluid(at, fluid_source, fluid_diag, xa, xb, sib, mid, wall)

    def mine(x):
        return lax.dynamic_slice_in_dim(x, gy * 12, 12, axis=1)

    displacement = last(s1, got2, stiff_ref, mine(f1), mine(w1), mine(f2), mine(w2)).reshape(3, 3072)
    return pressure, displacement


def solution(mesh):
    in_specs = (
        P("gx", "gy", None),
        P("gx", "gy", None),
        P(),
        P(("gx", "gy")),
        P(None, ("gx", "gy")),
        P(("gx", "gy")),
        P(("gx", "gy")),
        P(None, ("gx", "gy")),
        P(None, ("gx", "gy")),
        P(None, ("gx", "gy")),
        P(None, ("gx", "gy")),
        P(None, "gx", "gy"),
        P(None, "gx", "gy"),
    )
    out_specs = (P("gx", "gy", None), P(None, ("gx", "gy")))
    return jax.shard_map(local, mesh=mesh, in_specs=in_specs, out_specs=out_specs, check_vma=False)
```

```python
import functools

import jax
import jax.numpy as jnp
from jax import lax
from jax.experimental import pallas as pl
from jax.experimental.pallas import tpu as pltpu
from jax.sharding import PartitionSpec as P

F32 = jnp.float32
BF = jnp.bfloat16
AXES = ("gx", "gy")
N_GX = 32
N_DEV = 128
LR = 64
VR = 56
OWN = 48
CORE = 1
YHI = 2

pseudo_weight = 0.8
traction_scale = 30.0
motion_scale = 2.0
relax_weight = 0.5

VM = pl.BlockSpec(memory_space=pltpu.VMEM)
SM = pl.BlockSpec(memory_space=pltpu.SMEM)


def params(mib=40):
    return pltpu.CompilerParams(vmem_limit_bytes=mib << 20)


def swap(x, mask):
    return lax.ppermute(x, AXES, [(i, i ^ mask) for i in range(N_DEV)])


def from_gx(x, by):
    return lax.ppermute(x, "gx", [(i, i + by) for i in range(N_GX) if 0 <= i + by < N_GX])


def from_gy(x, by):
    return lax.ppermute(x, "gy", [(i, i + by) for i in range(4) if 0 <= i + by < 4])


def split(v):
    hi = v.astype(BF)
    return hi, (v - hi.astype(F32)).astype(BF)


def scale_of(stiff_ref):
    r = lax.broadcasted_iota(jnp.int32, (81, 81), 0)
    c = lax.broadcasted_iota(jnp.int32, (81, 81), 1)
    diag = jnp.where(r == c, stiff_ref[...], 0.0)
    trace = diag.sum(axis=1, keepdims=True).sum(axis=0, keepdims=True)
    return 1.0 / jnp.maximum(1.0, trace)


def fill_stiff(stiff_ref, s_scr):
    s_scr[...] = jnp.zeros_like(s_scr)
    hi, lo = split(jnp.pad(stiff_ref[...] * scale_of(stiff_ref), ((0, 15), (0, 7))))
    s_scr[0:96, :] = hi
    s_scr[96:192, :] = lo


def fill_table(v_ref, t_scr):
    for c in range(3):
        v = jnp.concatenate([v_ref[c], jnp.zeros((LR - VR, 256), F32)], axis=0)
        hi, lo = split(v)
        t_scr[c * LR : (c + 1) * LR, 0:256] = hi
        t_scr[c * LR : (c + 1) * LR, 256:512] = lo


def block_of(b):
    return pl.ds(pl.multiple_of(b * 128, 128), 128)


def forces_of(x, s_scr, coef_ref, live, b):
    xh, xl = split(x)
    r = jnp.dot(s_scr[...], xh, preferred_element_type=F32)
    prod = r[:88] + r[96:184] + jnp.dot(s_scr[0:96, :], xl, preferred_element_type=F32)[:88]
    slot = lax.broadcasted_iota(jnp.int32, (1, 128), 1) + b * 128
    return prod * jnp.where(slot < live, coef_ref[:, block_of(b)], 0.0)


def apply_body(live_ref, v_ref, conn_ref, coef_ref, stiff_ref, out_ref, t_scr, s_scr, oh_scr, ml_scr, x_scr, a_scr, acc):
    fill_table(v_ref, t_scr)
    fill_stiff(stiff_ref, s_scr)
    x_scr[80:88, :] = jnp.zeros((8, 128), F32)
    acc[...] = jnp.zeros_like(acc)
    b256 = lax.broadcasted_iota(jnp.int32, (256, 128), 0).astype(F32).astype(BF)
    b64 = b256[:LR]
    one, nil = jnp.ones((256, 128), BF), jnp.zeros((256, 128), BF)
    oh_scr[:, 27 * 128 :] = jnp.zeros((256, 128), BF)
    ml_scr[:, 27 * 128 :] = jnp.zeros((LR, 128), BF)
    a_scr[:, 27 * 128 :] = jnp.zeros((384, 128), BF)
    live = live_ref[0]

    def block(b, carry):
        for p in range(14):
            for h in range(2):
                k = 2 * p + h
                if k < 27:
                    sl = slice(k * 128, k * 128 + 128)
                    idx = conn_ref[k : k + 1, block_of(b)]
                    oh_scr[:, sl] = jnp.where(b256 == (idx & 255).astype(F32).astype(BF), one, nil)
                    ml_scr[:, sl] = jnp.where(b64 == (idx >> 8).astype(F32).astype(BF), one[:LR], nil[:LR])
            sp = slice(p * 256, p * 256 + 256)
            oh = oh_scr[:, sp]
            g = jnp.dot(t_scr[...], jnp.concatenate([oh, oh], axis=0), preferred_element_type=F32)
            m = ml_scr[:, sp].astype(F32)
            for c in range(3):
                s = (g[c * LR : (c + 1) * LR] * m).sum(axis=0, keepdims=True)
                for h in range(2):
                    k = 2 * p + h
                    if k < 27:
                        x_scr[c * 27 + k : c * 27 + k + 1, :] = s[:, h * 128 : h * 128 + 128]
        prod = forces_of(x_scr[...], s_scr, coef_ref, live, b)
        ph = prod.astype(BF).astype(F32)
        parts = (ph, prod - ph)
        for k in range(27):
            sl = slice(k * 128, k * 128 + 128)
            m = ml_scr[:, sl].reshape(4, 16, 128)
            for c in range(3):
                row = c * 27 + k
                for j, src in enumerate(parts):
                    r16 = jnp.broadcast_to(src[row : row + 1, :], (16, 128)).astype(BF)
                    at = j * 192 + c * LR
                    a_scr[at : at + LR, sl] = (m * r16[None]).reshape(LR, 128)
        acc[...] += lax.dot_general(
            a_scr[...], oh_scr[...], (((1,), (1,)), ((), ())), preferred_element_type=F32
        )
        return carry

    lax.fori_loop(0, (live + 127) // 128, block, 0)
    for c in range(3):
        s = acc[c * LR : (c + 1) * LR, :] + acc[192 + c * LR : 192 + (c + 1) * LR, :]
        out_ref[c] = s[:VR]


def stiff_apply(live, v, conn, coef, stiff):
    return pl.pallas_call(
        apply_body,
        out_shape=jax.ShapeDtypeStruct((3, VR, 256), F32),
        in_specs=[SM] + [VM] * 4,
        out_specs=VM,
        scratch_shapes=[
            pltpu.VMEM((192, 512), BF),
            pltpu.VMEM((192, 88), BF),
            pltpu.VMEM((256, 3584), BF),
            pltpu.VMEM((LR, 3584), BF),
            pltpu.VMEM((88, 128), F32),
            pltpu.VMEM((384, 3584), BF),
            pltpu.VMEM((384, 256), F32),
        ],
        compiler_params=params(),
        cost_estimate=pl.CostEstimate(flops=6 * 10**9, bytes_accessed=24 * 10**6, transcendentals=0),
    )(live, v, conn, coef, stiff)


def pack_parts_body(stiff_ref, load_ref, mass_ref, face_ref, tw_ref, normal_ref, out_ref):
    def put(at, row):
        out_ref[at : at + 1, :] = row[:, :128]
        out_ref[64 + at : 65 + at, :] = row[:, 128:]

    scale = scale_of(stiff_ref)
    for r in range(12):
        sl = slice(r * 256, r * 256 + 256)
        for c in range(3):
            put(c * 12 + r, load_ref[c : c + 1, sl])
        put(36 + r, mass_ref[:, sl] * scale)
    for k in range(4):
        put(48 + k, face_ref[k : k + 1, :].astype(F32))
        put(52 + k, tw_ref[k : k + 1, :])
    for c in range(3):
        put(56 + c, normal_ref[c : c + 1, :])
    zero = jnp.zeros((1, 256), F32)
    for r in range(59, 64):
        put(r, zero)


def pack_parts(stiff, load, mass, face, weight, normal):
    return pl.pallas_call(
        pack_parts_body,
        out_shape=jax.ShapeDtypeStruct((128, 128), F32),
        in_specs=[VM] * 6,
        out_specs=VM,
        compiler_params=params(),
    )(stiff, load, mass, face, weight, normal)


def pack_wall_body(at_ref, fs_ref, fd_ref, xa_ref, xb_ref, node_ref, ww_ref, out_ref):
    out_ref[...] = jnp.zeros_like(out_ref)
    even = jnp.full((32, 128), at_ref[0] & 1, jnp.int32) == 0
    for j, ref in enumerate((fs_ref, fd_ref)):
        for x in range(14):
            if x < 3:
                v = jnp.where(even, xb_ref[j, x], xa_ref[j, x])
            elif x < 11:
                v = ref[x - 3]
            else:
                v = jnp.where(even, xa_ref[j, x - 11], xb_ref[j, x - 11])
            t = v.T
            for z in range(4):
                at = j * 64 + z * 16 + x
                out_ref[at : at + 1, 0:32] = t[z : z + 1, :]
    for k in range(4):
        out_ref[128 + k * 8 : 136 + k * 8, 0:32] = node_ref[k].astype(F32)
        out_ref[160 + k * 8 : 168 + k * 8, 0:32] = ww_ref[k]
    out_ref[...] = pltpu.roll(out_ref[...], at_ref[1] * 32, 1)


def pack_wall(at, fs, fd, xa, xb, node, weight):
    def block(*shape):
        return pl.BlockSpec(shape, lambda i: (0,) * len(shape))

    return pl.pallas_call(
        pack_wall_body,
        grid=(1,),
        out_shape=jax.ShapeDtypeStruct((192, 128), F32),
        in_specs=[
            SM,
            block(8, 32, 128),
            block(8, 32, 128),
            block(2, 3, 32, 128),
            block(2, 3, 32, 128),
            block(4, 8, 32),
            block(4, 8, 32),
        ],
        out_specs=block(192, 128),
        compiler_params=params(),
    )(at, fs, fd, xa, xb, node, weight)


def source_of(vec_ref, seg_ref, pick_ref):
    rows = []
    for g in range(4):
        total = jnp.zeros((1, 256), F32)
        for c in range(3):
            total = total + seg_ref[g, 8 + c : 9 + c, :] * vec_ref[c, 12 * g : 12 * g + 1, :]
        rows.append(total)
    return split(jnp.concatenate(rows + [jnp.zeros((4, 256), F32)], axis=0))


def settle_body(*refs, first):
    at_ref, live_ref, p_ref, q_ref, edge_ref, mass_ref, v_ref, conn_ref, coef_ref, stiff_ref = refs[:10]
    if first:
        seg_ref, pick_ref, w_ref, out_ref, ws_ref = refs[10:15]
    else:
        w_ref, out_ref = refs[10:12]
    t_scr, s_scr, x_scr, acc = refs[-4:]
    keep = lax.broadcasted_iota(jnp.int32, (VR, 256), 0)
    end = jnp.where(at_ref[0] == N_GX - 1, OWN, OWN + 1)
    mask = (keep < end).astype(F32)
    mass = mass_ref[...]
    dots = [jnp.zeros((8, 256), F32) for _ in range(4)]
    for c in range(3):
        v = v_ref[c]
        w = p_ref[c] + q_ref[c]
        w = w + jnp.where(keep == 0, edge_ref[0, c : c + 1, :], jnp.where(keep == OWN, edge_ref[1, c : c + 1, :], 0.0))
        w = (w + mass * v) * mask
        w_ref[c] = w
        for i, (x, y) in enumerate(((v, v), (v, w), (w, w), (w, mass * w))):
            dots[i] = dots[i] + (x[:OWN] * y[:OWN]).reshape(6, 8, 256).sum(axis=0)
    dots = [0.25 * d.sum(axis=0, keepdims=True).sum(axis=1, keepdims=True) for d in dots]

    if first:
        hf, lf = source_of(v_ref, seg_ref, pick_ref)
        hw, lw = source_of(w_ref, seg_ref, pick_ref)
        table = jnp.concatenate([hf, lf, hw, lw], axis=0)
        n256 = lax.broadcasted_iota(jnp.int32, (256, 128), 0)
        n8 = lax.broadcasted_iota(jnp.int32, (8, 128), 0)
        for x in range(8):
            tf = jnp.zeros((8, 128), F32)
            tw = jnp.zeros((8, 128), F32)
            for k in range(4):
                row = k * 8 + x
                node = pick_ref[row : row + 1, :].astype(jnp.int32)
                oh = (n256 == (node & 255)).astype(F32).astype(BF)
                r = jnp.dot(table, oh, preferred_element_type=F32)
                u = jnp.where(n8 == (node >> 8), pick_ref[32 + row : 33 + row, :], 0.0)
                tf = tf + (r[0:8] + r[8:16]) * u
                tw = tw + (r[16:24] + r[24:32]) * u
            ws_ref[x : x + 1, :] = (motion_scale * relax_weight) * tf.sum(axis=0, keepdims=True)
            ws_ref[8 + x : 9 + x, :] = (motion_scale * relax_weight) * tw.sum(axis=0, keepdims=True)

    fill_table(w_ref, t_scr)
    fill_stiff(stiff_ref, s_scr)
    acc[...] = jnp.zeros_like(acc)
    x_scr[80:88, :] = jnp.zeros((8, 128), F32)
    b256 = lax.broadcasted_iota(jnp.int32, (256, 128), 0).astype(F32).astype(BF)
    one, nil = jnp.ones((256, 128), BF), jnp.zeros((256, 128), BF)
    i64 = lax.broadcasted_iota(jnp.int32, (LR, 128), 0)
    live = live_ref[0]

    def block(b, carry):
        for p in range(14):
            pieces, masks = [], []
            for k in (2 * p, 2 * p + 1):
                idx = conn_ref[min(k, 26) : min(k, 26) + 1, block_of(b)]
                pieces.append(jnp.where(b256 == (idx & 255).astype(F32).astype(BF), one, nil))
                masks.append((i64 == (idx >> 8)).astype(F32))
            oh = jnp.concatenate(pieces, axis=1)
            g = jnp.dot(t_scr[...], jnp.concatenate([oh, oh], axis=0), preferred_element_type=F32)
            m = jnp.concatenate(masks, axis=1)
            for c in range(3):
                s = (g[c * LR : (c + 1) * LR] * m).sum(axis=0, keepdims=True)
                for h in range(2):
                    k = 2 * p + h
                    if k < 27:
                        x_scr[c * 27 + k : c * 27 + k + 1, :] = s[:, h * 128 : h * 128 + 128]
        x = x_scr[...]
        acc[...] += (forces_of(x, s_scr, coef_ref, live, b) * x).sum(axis=0, keepdims=True)
        return carry

    lax.fori_loop(0, (live + 127) // 128, block, 0)
    dots[3] = dots[3] + acc[...].sum(axis=1, keepdims=True)
    lane = lax.broadcasted_iota(jnp.int32, (1, 128), 1)
    row = jnp.zeros((1, 128), F32)
    for i in range(4):
        row = jnp.where(lane == i, dots[i], row)
    row = jnp.broadcast_to(row, (N_DEV, 128))
    if first:
        peer = lax.broadcasted_iota(jnp.int32, (N_DEV, 128), 0) >> 2
        after = peer > at_ref[0]
        out_ref[pl.ds(0, N_DEV, 4), :] = row
        out_ref[pl.ds(1, N_DEV, 4), :] = jnp.where(after, ws_ref[7:8, :], ws_ref[0:1, :])
        out_ref[pl.ds(2, N_DEV, 4), :] = jnp.where(after, ws_ref[15:16, :], ws_ref[8:9, :])
        out_ref[pl.ds(3, N_DEV, 4), :] = jnp.zeros((N_DEV, 128), F32)
    else:
        out_ref[...] = row


def settle(at, live, p, q, edge, mass, v, conn, coef, stiff, wall=()):
    first = bool(wall)
    shapes = [(3, VR, 256), (4 * N_DEV, 128), (16, 128)] if first else [(3, VR, 256), (N_DEV, 128)]
    return pl.pallas_call(
        functools.partial(settle_body, first=first),
        out_shape=tuple(jax.ShapeDtypeStruct(x, F32) for x in shapes),
        in_specs=[SM, SM] + [VM] * (8 + len(wall)),
        out_specs=(VM,) * len(shapes),
        scratch_shapes=[
            pltpu.VMEM((192, 512), BF),
            pltpu.VMEM((192, 88), BF),
            pltpu.VMEM((88, 128), F32),
            pltpu.VMEM((1, 128), F32),
        ],
        compiler_params=params(),
        cost_estimate=pl.CostEstimate(flops=6 * 10**9, bytes_accessed=24 * 10**6, transcendentals=0),
    )(at, live, p, q, edge, mass, v, conn, coef, stiff, *wall)


def rows_in(at_ref):
    x = lax.broadcasted_iota(jnp.int32, (16, 128), 0) + at_ref[0] * 8 - 3
    return ((x >= 0) & (x < N_GX * 8)).astype(F32)


def wall_step(p, gain, force, inside, depth):
    lane = lax.broadcasted_iota(jnp.int32, (16, 128), 1)
    out = []
    for z in range(depth):
        c = p[z]
        n = pltpu.roll(c, 1, 0) + pltpu.roll(c, 15, 0)
        n = n + jnp.where(lane == 0, 0.0, pltpu.roll(c, 1, 1))
        n = n + jnp.where(lane == 127, 0.0, pltpu.roll(c, 127, 1))
        n = n + p[z + 1]
        if z > 0:
            n = n + p[z - 1]
        out.append(((1.0 - pseudo_weight) * c + gain[z] * (force[z] + n)) * inside)
    return out


def wall_front(at_ref, slab_ref):
    inside = rows_in(at_ref)
    fs = [slab_ref[z * 16 : z * 16 + 16, :] for z in range(4)]
    gain = [pseudo_weight / (6.0 + slab_ref[64 + z * 16 : 64 + z * 16 + 16, :]) for z in range(4)]
    p1 = [gain[z] * fs[z] * inside for z in range(4)]
    p2 = wall_step(p1, gain, fs, inside, 3)
    return inside, fs, gain, p2


def push(wall16, load_ref, seg_ref, f_ref):
    wall = pltpu.roll(wall16, 13, 0)[0:8]
    hi, lo = split(wall)
    table = jnp.concatenate([hi, lo], axis=0)
    i128 = lax.broadcasted_iota(jnp.int32, (128, 256), 0)
    i8 = lax.broadcasted_iota(jnp.int32, (8, 256), 0)
    f_ref[...] = load_ref[...]
    for g in range(4):
        total = jnp.zeros((8, 256), F32)
        for k in range(4):
            face = seg_ref[g, k : k + 1, :].astype(jnp.int32)
            oh = (i128 == ((face >> 8) * 32 + (face & 31))).astype(F32).astype(BF)
            r = jnp.dot(table, oh, preferred_element_type=F32)
            w = jnp.where(i8 == ((face >> 5) & 7), seg_ref[g, 4 + k : 5 + k, :], 0.0)
            total = total + (r[:8] + r[8:]) * w
        traction = total.sum(axis=0, keepdims=True)
        for c in range(3):
            f_ref[c, 12 * g : 12 * g + 1, :] = (
                f_ref[c, 12 * g : 12 * g + 1, :]
                + traction_scale * traction * seg_ref[g, 8 + c : 9 + c, :]
            )


def first_body(at_ref, slab_ref, load_ref, seg_ref, f_ref):
    inside, fs, gain, p2 = wall_front(at_ref, slab_ref)
    push(p2[0], load_ref, seg_ref, f_ref)


def first_force(at, slab, load, seg):
    return pl.pallas_call(
        first_body,
        out_shape=jax.ShapeDtypeStruct((3, VR, 256), F32),
        in_specs=[SM, VM, VM, VM],
        out_specs=VM,
        compiler_params=params(),
    )(at, slab, load, seg)


def weights_of(sums, stiff_ref):
    lane = lax.broadcasted_iota(jnp.int32, (1, 128), 1)
    a, b, c, d = [jnp.where(lane == i, sums, 0.0).sum(axis=1, keepdims=True) for i in range(4)]
    inv = scale_of(stiff_ref)
    alpha = a / b
    beta = (c - b * (b / a)) / (d - c * (c / b))
    return (alpha + beta * (alpha * (c / b))) * inv, -(alpha * beta) * inv


def second_body(at_ref, got_ref, stiff_ref, ws_ref, slab_ref, load_ref, seg_ref, f_ref, wall_ref, sums_ref):
    inside, fs, gain, p2 = wall_front(at_ref, slab_ref)
    sums = got_ref[pl.ds(0, N_DEV, 4), :].sum(axis=0, keepdims=True)
    sums_ref[...] = jnp.broadcast_to(sums, (8, 128))
    c0, c1 = weights_of(sums, stiff_ref)
    gx = at_ref[0]
    wall_ref[...] = jnp.zeros_like(wall_ref)
    wall_ref[3:11, :] = c0 * ws_ref[0:8, :] + c1 * ws_ref[8:16, :]
    for row, by, edge in ((2, -1, 0), (11, 1, N_GX - 1)):
        peer = jnp.clip(gx + by, 0, N_GX - 1) * 4 + at_ref[1]
        got = c0 * got_ref[pl.ds(peer * 4 + 1, 1), :] + c1 * got_ref[pl.ds(peer * 4 + 2, 1), :]
        wall_ref[row : row + 1, :] = jnp.where(jnp.full((1, 128), gx, jnp.int32) == edge, 0.0, got)
    force = [fs[0] + wall_ref[...], fs[1]]
    p3 = wall_step(p2, gain, force, inside, 2)
    p4 = wall_step(p3, gain, force, inside, 1)
    push(p4[0], load_ref, seg_ref, f_ref)


def second_force(at, got, stiff, ws, slab, load, seg):
    return pl.pallas_call(
        second_body,
        out_shape=(
            jax.ShapeDtypeStruct((3, VR, 256), F32),
            jax.ShapeDtypeStruct((16, 128), F32),
            jax.ShapeDtypeStruct((8, 128), F32),
        ),
        in_specs=[SM] + [VM] * 6,
        out_specs=(VM, VM, VM),
        compiler_params=params(),
    )(at, got, stiff, ws, slab, load, seg)


def fluid_body(at_ref, fs_ref, fd_ref, xa_ref, xb_ref, sib_ref, mid_ref, ws_ref, out_ref, src, gain, pa, pb):
    odd = jnp.full((4, 512), at_ref[1] & 1, jnp.int32) == 1
    even = jnp.full((32, 512), at_ref[0] & 1, jnp.int32) == 0
    zero = jnp.zeros((4, 512), F32)
    for j, (ref, dst) in enumerate(((fs_ref, src), (fd_ref, gain))):
        for x in range(14):
            if x < 3:
                own = jnp.where(even, xb_ref[j, x], xa_ref[j, x])
            elif x < 11:
                own = ref[x - 3]
            else:
                own = jnp.where(even, xa_ref[j, x - 11], xb_ref[j, x - 11])
            dst[x, 8:40, :] = own
            sib, mid = sib_ref[j, x], mid_ref[j, x]
            dst[x, 0:8, :] = jnp.concatenate([zero, jnp.where(odd, sib, mid)], axis=0)
            dst[x, 40:48, :] = jnp.concatenate([jnp.where(odd, mid, sib), zero], axis=0)
    lane = lax.broadcasted_iota(jnp.int32, (48, 512), 1)
    y = lax.broadcasted_iota(jnp.int32, (48, 512), 0) + at_ref[1] * 32 - 8
    y_in = ((y >= 0) & (y < 128)).astype(F32)

    def x_in(x):
        gx = at_ref[0] * 8 + x - 3
        return jnp.where((gx >= 0) & (gx < N_GX * 8), 1.0, 0.0).astype(F32)

    def start(x, carry):
        g = pseudo_weight / (6.0 + gain[x]) * (y_in * x_in(x))
        gain[x] = g
        pa[x] = g * src[x]
        return carry

    lax.fori_loop(0, 14, start, 0)

    def new_row(p, x):
        c = p[x]
        n = p[x - 1] + p[x + 1] + pltpu.roll(c, 1, 0) + pltpu.roll(c, 47, 0)
        n = n + jnp.where(lane == 0, 0.0, pltpu.roll(c, 1, 1))
        n = n + jnp.where(lane == 511, 0.0, pltpu.roll(c, 511, 1))
        return (1.0 - pseudo_weight) * c + gain[x] * (src[x] + n)

    def second(x, carry):
        pb[x] = new_row(pa, x)
        return carry

    lax.fori_loop(1, 13, second, 0)

    def add_source(x, carry):
        src[x, :, 0:128] = src[x, :, 0:128] + ws_ref[x]
        return carry

    lax.fori_loop(2, 12, add_source, 0)

    def third(x, carry):
        pa[x] = new_row(pb, x)
        return carry

    lax.fori_loop(2, 12, third, 0)

    def fourth(x, carry):
        out_ref[x - 3] = new_row(pa, x)[8:40]
        return carry

    lax.fori_loop(3, 11, fourth, 0)


def fluid(at, fs, fd, xa, xb, sib, mid, ws):
    return pl.pallas_call(
        fluid_body,
        out_shape=jax.ShapeDtypeStruct((8, 32, 512), F32),
        in_specs=[SM] + [VM] * 7,
        out_specs=VM,
        scratch_shapes=[pltpu.VMEM((14, 48, 512), F32)] * 4,
        compiler_params=params(),
        cost_estimate=pl.CostEstimate(flops=10**8, bytes_accessed=20 * 10**6, transcendentals=0),
    )(at, fs, fd, xa, xb, sib, mid, ws)


def last_body(s1_ref, got_ref, stiff_ref, f1_ref, w1_ref, f2_ref, w2_ref, out_ref):
    c0, c1 = weights_of(s1_ref[0:1, :], stiff_ref)
    d0, d1 = weights_of(got_ref[...].sum(axis=0, keepdims=True), stiff_ref)
    for c in range(3):
        before = relax_weight * (c0 * f1_ref[c] + c1 * w1_ref[c])
        solved = d0 * f2_ref[c] + d1 * w2_ref[c]
        new = before + relax_weight * (solved - before)
        for r in range(12):
            out_ref[c : c + 1, r * 256 : r * 256 + 256] = new[r : r + 1, :]


def last(s1, got, stiff, f1, w1, f2, w2):
    return pl.pallas_call(
        last_body,
        out_shape=jax.ShapeDtypeStruct((3, 3072), F32),
        in_specs=[VM] * 7,
        out_specs=VM,
        compiler_params=params(),
    )(s1, got, stiff, f1, w1, f2, w2)


def local(
    fluid_source,
    fluid_diag,
    stiff_ref,
    elem_coef,
    connect,
    live_count,
    node_mass,
    solid_load,
    wet_normal,
    trac_face,
    trac_weight,
    wall_node,
    wall_weight,
):
    gx = lax.axis_index("gx")
    gy = lax.axis_index("gy")
    core = gy & 1
    yhi = gy >> 1
    at = jnp.stack([gx, gy]).astype(jnp.int32)

    def in_order(bit, own, other):
        return jnp.concatenate([jnp.where(bit == 0, own, other), jnp.where(bit == 0, other, own)], axis=0)

    even = gx % 2 == 0
    low_pairs = [(i, i ^ 1) for i in range(N_GX)]
    high_pairs = [(i, i + 1) for i in range(1, N_GX - 1, 2)]
    high_pairs = high_pairs + [(j, i) for i, j in high_pairs]

    def beside(to_low, to_high, cross=False):
        sends = jnp.where(even, to_high, to_low), jnp.where(even, to_low, to_high)
        got = []
        for send, pairs in zip(sends, (low_pairs, high_pairs)):
            if cross:
                both_ends = [(4 * i + g, 4 * j + (g ^ (2 * (g & 1)))) for i, j in pairs for g in range(4)]
                got.append(lax.ppermute(send, AXES, both_ends))
            else:
                got.append(lax.ppermute(send, "gx", pairs))
        return got

    def three(part):
        return jnp.stack([fluid_source[part], fluid_diag[part]])

    sa, sb = beside(three(slice(0, 3))[..., :128], three(slice(5, 8))[..., :128])

    own = pack_parts(
        stiff_ref, solid_load, node_mass.reshape(1, 3072), trac_face, trac_weight, wet_normal
    )
    wide = pack_wall(at, fluid_source, fluid_diag, sa, sb, wall_node, wall_weight)
    near = swap(jnp.concatenate([own, wide], axis=0), CORE)
    pair = jnp.concatenate([in_order(core, own, near[:128]), wide + near[128:]], axis=0)
    far = swap(pair, YHI)
    wide = pair[256:] + far[256:]
    slab, pick = wide[:128], wide[128:]
    parts = in_order(yhi, pair[:256], far[:256]).reshape(4, 2, 64, 128)
    parts = jnp.concatenate([parts[:, 0], parts[:, 1]], axis=2)
    seg = parts[:, 48:64]
    load = parts[:, :36].reshape(4, 3, 12, 256).transpose(1, 0, 2, 3).reshape(3, OWN, 256)
    load = jnp.pad(load, ((0, 0), (0, VR - OWN), (0, 0)))
    mass = jnp.pad(parts[:, 36:48].reshape(OWN, 256), ((0, VR - OWN), (0, 0)))
    coef = elem_coef.reshape(1, 384)
    row = lax.broadcasted_iota(jnp.int32, (3, VR, 256), 1)

    def to_all(x):
        return lax.all_to_all(x, AXES, 0, 0, tiled=True)

    def exchange(s):
        pair = s + swap(s, CORE)
        far = swap(pair, YHI)
        ab = beside(pair[:, 0, :], pair[:, OWN, :], cross=True)
        return pair, far, ab

    def edges(far, ab):
        far, (a, b) = lax.optimization_barrier((far, ab))
        got = jnp.stack([jnp.where(even, b, a), jnp.where(even, a, b)])
        return far, got + swap(got, CORE)

    f1 = first_force(at, slab, load, seg)
    following = from_gx(jnp.concatenate([f1[:, 0, :], mass[0:1]], axis=0), -1)
    f1 = jnp.where(row == OWN, following[0:3, None, :], f1)
    mass = jnp.where(row[0] == OWN, following[3:4], mass)

    pair1, far1, ab = exchange(stiff_apply(live_count, f1, connect, coef, stiff_ref))
    far1, edge1 = edges(far1, ab)
    w1, out1, wsb = settle(
        at, live_count, pair1, far1, edge1, mass, f1, connect, coef, stiff_ref, (seg, pick)
    )
    rows, out1 = lax.optimization_barrier(((three(slice(0, 3)), three(slice(5, 8))), out1))
    got1 = to_all(out1)
    xa, xb = beside(*rows)
    f2, ws, s1 = second_force(at, got1, stiff_ref, wsb, slab, load, seg)
    following = from_gx(f2[:, 0, :], -1)
    f2 = jnp.where(row == OWN, following[:, None, :], f2)
    f2, xa, xb = lax.optimization_barrier((f2, xa, xb))
    pair2, far2, ab = exchange(stiff_apply(live_count, f2, connect, coef, stiff_ref))

    xlo, xhi = jnp.where(even, xb, xa), jnp.where(even, xa, xb)

    def columns(part):
        middle = jnp.stack([fluid_source[:, part], fluid_diag[:, part]])
        return jnp.concatenate([xlo[:, :, part], middle, xhi[:, :, part]], axis=1)

    low, high = columns(slice(0, 4)), columns(slice(28, 32))
    sides = (jnp.where(core == 0, high, low), jnp.where(core == 0, low, high))
    padded = jnp.pad(ws, ((0, 0), (8, 8)))
    wall = lax.dynamic_slice_in_dim(padded, gy * 32, 48, axis=1)
    lane = lax.broadcasted_iota(jnp.int32, (16, 48, 128), 2)
    wall = jnp.where(lane == 0, wall[:, :, None], 0.0)
    sides, wall, pair2 = lax.optimization_barrier((sides, wall, pair2))
    far2, edge2 = edges(far2, ab)
    sides, far2, edge2 = lax.optimization_barrier((sides, far2, edge2))
    sib = swap(sides[0], CORE)
    mid = lax.ppermute(sides[1], "gy", [(1, 2), (2, 1)])
    w2, out2 = settle(at, live_count, pair2, far2, edge2, mass, f2, connect, coef, stiff_ref)
    out2, sib, mid = lax.optimization_barrier((out2, sib, mid))
    got2 = to_all(out2)
    pressure = fluid(at, fluid_source, fluid_diag, xa, xb, sib, mid, wall)

    def mine(x):
        return lax.dynamic_slice_in_dim(x, gy * 12, 12, axis=1)

    displacement = last(s1, got2, stiff_ref, mine(f1), mine(w1), mine(f2), mine(w2))
    return pressure, displacement


def solution(mesh):
    in_specs = (
        P("gx", "gy", None),
        P("gx", "gy", None),
        P(),
        P(("gx", "gy")),
        P(None, ("gx", "gy")),
        P(("gx", "gy")),
        P(("gx", "gy")),
        P(None, ("gx", "gy")),
        P(None, ("gx", "gy")),
        P(None, ("gx", "gy")),
        P(None, ("gx", "gy")),
        P(None, "gx", "gy"),
        P(None, "gx", "gy"),
    )
    out_specs = (P("gx", "gy", None), P(None, ("gx", "gy")))
    return jax.shard_map(local, mesh=mesh, in_specs=in_specs, out_specs=out_specs, check_vma=False)
```

```python
import functools

import jax
import jax.numpy as jnp
from jax import lax
from jax.experimental import pallas as pl
from jax.experimental.pallas import tpu as pltpu
from jax.sharding import PartitionSpec as P

F32 = jnp.float32
BF = jnp.bfloat16
AXES = ("gx", "gy")
N_GX = 32
N_DEV = 128
LR = 64
VR = 56
OWN = 48
CORE = 1
YHI = 2

pseudo_weight = 0.8
traction_scale = 30.0
motion_scale = 2.0
relax_weight = 0.5

VM = pl.BlockSpec(memory_space=pltpu.VMEM)
SM = pl.BlockSpec(memory_space=pltpu.SMEM)


def params(mib=40):
    return pltpu.CompilerParams(vmem_limit_bytes=mib << 20)


def swap(x, mask):
    return lax.ppermute(x, AXES, [(i, i ^ mask) for i in range(N_DEV)])


def from_gx(x, by):
    return lax.ppermute(x, "gx", [(i, i + by) for i in range(N_GX) if 0 <= i + by < N_GX])


def from_gy(x, by):
    return lax.ppermute(x, "gy", [(i, i + by) for i in range(4) if 0 <= i + by < 4])


def split(v):
    hi = v.astype(BF)
    return hi, (v - hi.astype(F32)).astype(BF)


def scale_of(stiff_ref):
    r = lax.broadcasted_iota(jnp.int32, (81, 81), 0)
    c = lax.broadcasted_iota(jnp.int32, (81, 81), 1)
    diag = jnp.where(r == c, stiff_ref[...], 0.0)
    trace = diag.sum(axis=1, keepdims=True).sum(axis=0, keepdims=True)
    return 1.0 / jnp.maximum(1.0, trace)


def fill_stiff(stiff_ref, s_scr):
    s_scr[...] = jnp.zeros_like(s_scr)
    hi, lo = split(jnp.pad(stiff_ref[...] * scale_of(stiff_ref), ((0, 15), (0, 7))))
    s_scr[0:96, :] = hi
    s_scr[96:192, :] = lo


def fill_table(v_ref, t_scr):
    blocks = [v_ref[c, 0:OWN, :] for c in range(3)] + [v_ref[c, OWN : OWN + 1, :] for c in range(3)]
    hi, lo = split(jnp.concatenate(blocks + [jnp.zeros((13, 256), F32)], axis=0))
    t_scr[:, 0:256] = hi
    t_scr[:, 256:512] = lo


def select_rows(g, m, c):
    s = (g[c * OWN : (c + 1) * OWN] * m[:OWN]).sum(axis=0, keepdims=True)
    return s + g[144 + c : 145 + c] * m[OWN : OWN + 1]


def block_of(b):
    return pl.ds(pl.multiple_of(b * 128, 128), 128)


def forces_of(x, s_scr, coef_ref, live, b):
    xh, xl = split(x)
    r = jnp.dot(s_scr[...], xh, preferred_element_type=F32)
    prod = r[:88] + r[96:184] + jnp.dot(s_scr[0:96, :], xl, preferred_element_type=F32)[:88]
    slot = lax.broadcasted_iota(jnp.int32, (1, 128), 1) + b * 128
    return prod * jnp.where(slot < live, coef_ref[:, block_of(b)], 0.0)


def apply_body(live_ref, v_ref, conn_ref, coef_ref, stiff_ref, out_ref, t_scr, s_scr, oh_scr, ml_scr, x_scr, a_scr, acc):
    fill_table(v_ref, t_scr)
    fill_stiff(stiff_ref, s_scr)
    x_scr[80:88, :] = jnp.zeros((8, 128), F32)
    acc[...] = jnp.zeros_like(acc)
    b256 = lax.broadcasted_iota(jnp.int32, (256, 128), 0).astype(F32).astype(BF)
    b64 = b256[:LR]
    one, nil = jnp.ones((256, 128), BF), jnp.zeros((256, 128), BF)
    oh_scr[:, 27 * 128 :] = jnp.zeros((256, 128), BF)
    ml_scr[:, 27 * 128 :] = jnp.zeros((LR, 128), BF)
    a_scr[:, 27 * 128 :] = jnp.zeros((320, 128), BF)
    live = live_ref[0]

    def block(b, carry):
        for p in range(14):
            for h in range(2):
                k = 2 * p + h
                if k < 27:
                    sl = slice(k * 128, k * 128 + 128)
                    idx = conn_ref[k : k + 1, block_of(b)]
                    oh_scr[:, sl] = jnp.where(b256 == (idx & 255).astype(F32).astype(BF), one, nil)
                    ml_scr[:, sl] = jnp.where(b64 == (idx >> 8).astype(F32).astype(BF), one[:LR], nil[:LR])
            sp = slice(p * 256, p * 256 + 256)
            oh = oh_scr[:, sp]
            g = jnp.dot(t_scr[...], jnp.concatenate([oh, oh], axis=0), preferred_element_type=F32)
            m = ml_scr[:, sp].astype(F32)
            for c in range(3):
                s = select_rows(g, m, c)
                for h in range(2):
                    k = 2 * p + h
                    if k < 27:
                        x_scr[c * 27 + k : c * 27 + k + 1, :] = s[:, h * 128 : h * 128 + 128]
        prod = forces_of(x_scr[...], s_scr, coef_ref, live, b)
        ph = prod.astype(BF).astype(F32)
        parts = (ph, prod - ph)
        for k in range(27):
            sl = slice(k * 128, k * 128 + 128)
            m = ml_scr[0:OWN, sl].reshape(3, 16, 128)
            last_row = ml_scr[OWN : OWN + 16, sl].astype(F32)[0:1]
            for j, src in enumerate(parts):
                rows = [src[c * 27 + k : c * 27 + k + 1, :] for c in range(3)]
                for c in range(3):
                    r16 = jnp.broadcast_to(rows[c], (16, 128)).astype(BF)
                    at = j * 160 + c * OWN
                    a_scr[at : at + OWN, sl] = (m * r16[None]).reshape(OWN, 128)
                tail = jnp.concatenate(rows + [jnp.zeros((13, 128), F32)], axis=0) * last_row
                a_scr[j * 160 + 144 : j * 160 + 160, sl] = tail.astype(BF)
        acc[...] += lax.dot_general(
            a_scr[...], oh_scr[...], (((1,), (1,)), ((), ())), preferred_element_type=F32
        )
        return carry

    lax.fori_loop(0, (live + 127) // 128, block, 0)
    for c in range(3):
        at = c * OWN
        out_ref[c, 0:OWN, :] = acc[at : at + OWN, :] + acc[160 + at : 160 + at + OWN, :]
        tail = acc[144 + c : 145 + c, :] + acc[304 + c : 305 + c, :]
        out_ref[c, OWN:VR, :] = jnp.concatenate([tail, jnp.zeros((VR - OWN - 1, 256), F32)], axis=0)


def stiff_apply(live, v, conn, coef, stiff):
    return pl.pallas_call(
        apply_body,
        out_shape=jax.ShapeDtypeStruct((3, VR, 256), F32),
        in_specs=[SM] + [VM] * 4,
        out_specs=VM,
        scratch_shapes=[
            pltpu.VMEM((160, 512), BF),
            pltpu.VMEM((192, 88), BF),
            pltpu.VMEM((256, 3584), BF),
            pltpu.VMEM((LR, 3584), BF),
            pltpu.VMEM((88, 128), F32),
            pltpu.VMEM((320, 3584), BF),
            pltpu.VMEM((320, 256), F32),
        ],
        compiler_params=params(),
        cost_estimate=pl.CostEstimate(flops=6 * 10**9, bytes_accessed=24 * 10**6, transcendentals=0),
    )(live, v, conn, coef, stiff)


def pack_parts_body(stiff_ref, load_ref, mass_ref, face_ref, tw_ref, normal_ref, out_ref):
    def put(at, row):
        out_ref[at : at + 1, :] = row[:, :128]
        out_ref[64 + at : 65 + at, :] = row[:, 128:]

    scale = scale_of(stiff_ref)
    for r in range(12):
        sl = slice(r * 256, r * 256 + 256)
        for c in range(3):
            put(c * 12 + r, load_ref[c : c + 1, sl])
        put(36 + r, mass_ref[:, sl] * scale)
    for k in range(4):
        put(48 + k, face_ref[k : k + 1, :].astype(F32))
        put(52 + k, tw_ref[k : k + 1, :])
    for c in range(3):
        put(56 + c, normal_ref[c : c + 1, :])
    zero = jnp.zeros((1, 256), F32)
    for r in range(59, 64):
        put(r, zero)


def pack_parts(stiff, load, mass, face, weight, normal):
    return pl.pallas_call(
        pack_parts_body,
        out_shape=jax.ShapeDtypeStruct((128, 128), F32),
        in_specs=[VM] * 6,
        out_specs=VM,
        compiler_params=params(),
    )(stiff, load, mass, face, weight, normal)


def pack_wall_body(at_ref, fs_ref, fd_ref, xa_ref, xb_ref, node_ref, ww_ref, out_ref):
    out_ref[...] = jnp.zeros_like(out_ref)
    even = jnp.full((32, 128), at_ref[0] & 1, jnp.int32) == 0
    for j, ref in enumerate((fs_ref, fd_ref)):
        for x in range(14):
            if x < 3:
                v = jnp.where(even, xb_ref[j, x], xa_ref[j, x])
            elif x < 11:
                v = ref[x - 3]
            else:
                v = jnp.where(even, xa_ref[j, x - 11], xb_ref[j, x - 11])
            t = v.T
            for z in range(4):
                at = j * 64 + z * 16 + x
                out_ref[at : at + 1, 0:32] = t[z : z + 1, :]
    for k in range(4):
        out_ref[128 + k * 8 : 136 + k * 8, 0:32] = node_ref[k].astype(F32)
        out_ref[160 + k * 8 : 168 + k * 8, 0:32] = ww_ref[k]
    out_ref[...] = pltpu.roll(out_ref[...], at_ref[1] * 32, 1)


def pack_wall(at, fs, fd, xa, xb, node, weight):
    def block(*shape):
        return pl.BlockSpec(shape, lambda i: (0,) * len(shape))

    return pl.pallas_call(
        pack_wall_body,
        grid=(1,),
        out_shape=jax.ShapeDtypeStruct((192, 128), F32),
        in_specs=[
            SM,
            block(8, 32, 128),
            block(8, 32, 128),
            block(2, 3, 32, 128),
            block(2, 3, 32, 128),
            block(4, 8, 32),
            block(4, 8, 32),
        ],
        out_specs=block(192, 128),
        compiler_params=params(),
    )(at, fs, fd, xa, xb, node, weight)


def source_of(vec_ref, seg_ref, pick_ref):
    rows = []
    for g in range(4):
        total = jnp.zeros((1, 256), F32)
        for c in range(3):
            total = total + seg_ref[g, 8 + c : 9 + c, :] * vec_ref[c, 12 * g : 12 * g + 1, :]
        rows.append(total)
    return split(jnp.concatenate(rows + [jnp.zeros((4, 256), F32)], axis=0))


def settle_body(*refs, first):
    at_ref, live_ref, p_ref, q_ref, edge_ref, mass_ref, v_ref, conn_ref, coef_ref, stiff_ref = refs[:10]
    if first:
        seg_ref, pick_ref, w_ref, out_ref, ws_ref = refs[10:15]
    else:
        w_ref, out_ref = refs[10:12]
    t_scr, s_scr, x_scr, acc = refs[-4:]
    keep = lax.broadcasted_iota(jnp.int32, (VR, 256), 0)
    end = jnp.where(at_ref[0] == N_GX - 1, OWN, OWN + 1)
    mask = (keep < end).astype(F32)
    mass = mass_ref[...]
    dots = [jnp.zeros((8, 256), F32) for _ in range(4)]
    for c in range(3):
        v = v_ref[c]
        w = p_ref[c] + q_ref[c]
        w = w + jnp.where(keep == 0, edge_ref[0, c : c + 1, :], jnp.where(keep == OWN, edge_ref[1, c : c + 1, :], 0.0))
        w = (w + mass * v) * mask
        w_ref[c] = w
        for i, (x, y) in enumerate(((v, v), (v, w), (w, w), (w, mass * w))):
            dots[i] = dots[i] + (x[:OWN] * y[:OWN]).reshape(6, 8, 256).sum(axis=0)
    dots = [0.25 * d.sum(axis=0, keepdims=True).sum(axis=1, keepdims=True) for d in dots]

    if first:
        hf, lf = source_of(v_ref, seg_ref, pick_ref)
        hw, lw = source_of(w_ref, seg_ref, pick_ref)
        table = jnp.concatenate([hf, lf, hw, lw], axis=0)
        n256 = lax.broadcasted_iota(jnp.int32, (256, 128), 0)
        n8 = lax.broadcasted_iota(jnp.int32, (8, 128), 0)
        for x in range(8):
            tf = jnp.zeros((8, 128), F32)
            tw = jnp.zeros((8, 128), F32)
            for k in range(4):
                row = k * 8 + x
                node = pick_ref[row : row + 1, :].astype(jnp.int32)
                oh = (n256 == (node & 255)).astype(F32).astype(BF)
                r = jnp.dot(table, oh, preferred_element_type=F32)
                u = jnp.where(n8 == (node >> 8), pick_ref[32 + row : 33 + row, :], 0.0)
                tf = tf + (r[0:8] + r[8:16]) * u
                tw = tw + (r[16:24] + r[24:32]) * u
            ws_ref[x : x + 1, :] = (motion_scale * relax_weight) * tf.sum(axis=0, keepdims=True)
            ws_ref[8 + x : 9 + x, :] = (motion_scale * relax_weight) * tw.sum(axis=0, keepdims=True)

    fill_table(w_ref, t_scr)
    fill_stiff(stiff_ref, s_scr)
    acc[...] = jnp.zeros_like(acc)
    x_scr[80:88, :] = jnp.zeros((8, 128), F32)
    b256 = lax.broadcasted_iota(jnp.int32, (256, 128), 0).astype(F32).astype(BF)
    one, nil = jnp.ones((256, 128), BF), jnp.zeros((256, 128), BF)
    i64 = lax.broadcasted_iota(jnp.int32, (LR, 128), 0)
    live = live_ref[0]

    def block(b, carry):
        for p in range(14):
            pieces, masks = [], []
            for k in (2 * p, 2 * p + 1):
                idx = conn_ref[min(k, 26) : min(k, 26) + 1, block_of(b)]
                pieces.append(jnp.where(b256 == (idx & 255).astype(F32).astype(BF), one, nil))
                masks.append((i64 == (idx >> 8)).astype(F32))
            oh = jnp.concatenate(pieces, axis=1)
            g = jnp.dot(t_scr[...], jnp.concatenate([oh, oh], axis=0), preferred_element_type=F32)
            m = jnp.concatenate(masks, axis=1)
            for c in range(3):
                s = select_rows(g, m, c)
                for h in range(2):
                    k = 2 * p + h
                    if k < 27:
                        x_scr[c * 27 + k : c * 27 + k + 1, :] = s[:, h * 128 : h * 128 + 128]
        x = x_scr[...]
        acc[...] += (forces_of(x, s_scr, coef_ref, live, b) * x).sum(axis=0, keepdims=True)
        return carry

    lax.fori_loop(0, (live + 127) // 128, block, 0)
    dots[3] = dots[3] + acc[...].sum(axis=1, keepdims=True)
    lane = lax.broadcasted_iota(jnp.int32, (1, 128), 1)
    row = jnp.zeros((1, 128), F32)
    for i in range(4):
        row = jnp.where(lane == i, dots[i], row)
    row = jnp.broadcast_to(row, (N_DEV, 128))
    if first:
        peer = lax.broadcasted_iota(jnp.int32, (N_DEV, 128), 0) >> 2
        after = peer > at_ref[0]
        out_ref[pl.ds(0, N_DEV, 4), :] = row
        out_ref[pl.ds(1, N_DEV, 4), :] = jnp.where(after, ws_ref[7:8, :], ws_ref[0:1, :])
        out_ref[pl.ds(2, N_DEV, 4), :] = jnp.where(after, ws_ref[15:16, :], ws_ref[8:9, :])
        out_ref[pl.ds(3, N_DEV, 4), :] = jnp.zeros((N_DEV, 128), F32)
    else:
        out_ref[...] = row


def settle(at, live, p, q, edge, mass, v, conn, coef, stiff, wall=()):
    first = bool(wall)
    shapes = [(3, VR, 256), (4 * N_DEV, 128), (16, 128)] if first else [(3, VR, 256), (N_DEV, 128)]
    return pl.pallas_call(
        functools.partial(settle_body, first=first),
        out_shape=tuple(jax.ShapeDtypeStruct(x, F32) for x in shapes),
        in_specs=[SM, SM] + [VM] * (8 + len(wall)),
        out_specs=(VM,) * len(shapes),
        scratch_shapes=[
            pltpu.VMEM((160, 512), BF),
            pltpu.VMEM((192, 88), BF),
            pltpu.VMEM((88, 128), F32),
            pltpu.VMEM((1, 128), F32),
        ],
        compiler_params=params(),
        cost_estimate=pl.CostEstimate(flops=6 * 10**9, bytes_accessed=24 * 10**6, transcendentals=0),
    )(at, live, p, q, edge, mass, v, conn, coef, stiff, *wall)


def rows_in(at_ref):
    x = lax.broadcasted_iota(jnp.int32, (16, 128), 0) + at_ref[0] * 8 - 3
    return ((x >= 0) & (x < N_GX * 8)).astype(F32)


def wall_step(p, gain, force, inside, depth):
    lane = lax.broadcasted_iota(jnp.int32, (16, 128), 1)
    out = []
    for z in range(depth):
        c = p[z]
        n = pltpu.roll(c, 1, 0) + pltpu.roll(c, 15, 0)
        n = n + jnp.where(lane == 0, 0.0, pltpu.roll(c, 1, 1))
        n = n + jnp.where(lane == 127, 0.0, pltpu.roll(c, 127, 1))
        n = n + p[z + 1]
        if z > 0:
            n = n + p[z - 1]
        out.append(((1.0 - pseudo_weight) * c + gain[z] * (force[z] + n)) * inside)
    return out


def wall_front(at_ref, slab_ref):
    inside = rows_in(at_ref)
    fs = [slab_ref[z * 16 : z * 16 + 16, :] for z in range(4)]
    gain = [pseudo_weight / (6.0 + slab_ref[64 + z * 16 : 64 + z * 16 + 16, :]) for z in range(4)]
    p1 = [gain[z] * fs[z] * inside for z in range(4)]
    p2 = wall_step(p1, gain, fs, inside, 3)
    return inside, fs, gain, p2


def push(wall16, load_ref, seg_ref, f_ref):
    wall = pltpu.roll(wall16, 13, 0)[0:8]
    hi, lo = split(wall)
    table = jnp.concatenate([hi, lo], axis=0)
    i128 = lax.broadcasted_iota(jnp.int32, (128, 256), 0)
    i8 = lax.broadcasted_iota(jnp.int32, (8, 256), 0)
    f_ref[...] = load_ref[...]
    for g in range(4):
        total = jnp.zeros((8, 256), F32)
        for k in range(4):
            face = seg_ref[g, k : k + 1, :].astype(jnp.int32)
            oh = (i128 == ((face >> 8) * 32 + (face & 31))).astype(F32).astype(BF)
            r = jnp.dot(table, oh, preferred_element_type=F32)
            w = jnp.where(i8 == ((face >> 5) & 7), seg_ref[g, 4 + k : 5 + k, :], 0.0)
            total = total + (r[:8] + r[8:]) * w
        traction = total.sum(axis=0, keepdims=True)
        for c in range(3):
            f_ref[c, 12 * g : 12 * g + 1, :] = (
                f_ref[c, 12 * g : 12 * g + 1, :]
                + traction_scale * traction * seg_ref[g, 8 + c : 9 + c, :]
            )


def first_body(at_ref, slab_ref, load_ref, seg_ref, f_ref):
    inside, fs, gain, p2 = wall_front(at_ref, slab_ref)
    push(p2[0], load_ref, seg_ref, f_ref)


def first_force(at, slab, load, seg):
    return pl.pallas_call(
        first_body,
        out_shape=jax.ShapeDtypeStruct((3, VR, 256), F32),
        in_specs=[SM, VM, VM, VM],
        out_specs=VM,
        compiler_params=params(),
    )(at, slab, load, seg)


def weights_of(sums, stiff_ref):
    lane = lax.broadcasted_iota(jnp.int32, (1, 128), 1)
    a, b, c, d = [jnp.where(lane == i, sums, 0.0).sum(axis=1, keepdims=True) for i in range(4)]
    inv = scale_of(stiff_ref)
    alpha = a / b
    beta = (c - b * (b / a)) / (d - c * (c / b))
    return (alpha + beta * (alpha * (c / b))) * inv, -(alpha * beta) * inv


def second_body(at_ref, got_ref, stiff_ref, ws_ref, slab_ref, load_ref, seg_ref, f_ref, wall_ref, sums_ref):
    inside, fs, gain, p2 = wall_front(at_ref, slab_ref)
    sums = got_ref[pl.ds(0, N_DEV, 4), :].sum(axis=0, keepdims=True)
    sums_ref[...] = jnp.broadcast_to(sums, (8, 128))
    c0, c1 = weights_of(sums, stiff_ref)
    gx = at_ref[0]
    wall_ref[...] = jnp.zeros_like(wall_ref)
    wall_ref[3:11, :] = c0 * ws_ref[0:8, :] + c1 * ws_ref[8:16, :]
    for row, by, edge in ((2, -1, 0), (11, 1, N_GX - 1)):
        peer = jnp.clip(gx + by, 0, N_GX - 1) * 4 + at_ref[1]
        got = c0 * got_ref[pl.ds(peer * 4 + 1, 1), :] + c1 * got_ref[pl.ds(peer * 4 + 2, 1), :]
        wall_ref[row : row + 1, :] = jnp.where(jnp.full((1, 128), gx, jnp.int32) == edge, 0.0, got)
    force = [fs[0] + wall_ref[...], fs[1]]
    p3 = wall_step(p2, gain, force, inside, 2)
    p4 = wall_step(p3, gain, force, inside, 1)
    push(p4[0], load_ref, seg_ref, f_ref)


def second_force(at, got, stiff, ws, slab, load, seg):
    return pl.pallas_call(
        second_body,
        out_shape=(
            jax.ShapeDtypeStruct((3, VR, 256), F32),
            jax.ShapeDtypeStruct((16, 128), F32),
            jax.ShapeDtypeStruct((8, 128), F32),
        ),
        in_specs=[SM] + [VM] * 6,
        out_specs=(VM, VM, VM),
        compiler_params=params(),
    )(at, got, stiff, ws, slab, load, seg)


def fluid_body(at_ref, fs_ref, fd_ref, xa_ref, xb_ref, sib_ref, mid_ref, ws_ref, out_ref, src, gain, pa, pb):
    odd = jnp.full((4, 512), at_ref[1] & 1, jnp.int32) == 1
    even = jnp.full((32, 512), at_ref[0] & 1, jnp.int32) == 0
    zero = jnp.zeros((4, 512), F32)
    for j, (ref, dst) in enumerate(((fs_ref, src), (fd_ref, gain))):
        for x in range(14):
            if x < 3:
                own = jnp.where(even, xb_ref[j, x], xa_ref[j, x])
            elif x < 11:
                own = ref[x - 3]
            else:
                own = jnp.where(even, xa_ref[j, x - 11], xb_ref[j, x - 11])
            dst[x, 8:40, :] = own
            sib, mid = sib_ref[j, x], mid_ref[j, x]
            dst[x, 0:8, :] = jnp.concatenate([zero, jnp.where(odd, sib, mid)], axis=0)
            dst[x, 40:48, :] = jnp.concatenate([jnp.where(odd, mid, sib), zero], axis=0)
    lane = lax.broadcasted_iota(jnp.int32, (48, 512), 1)
    y = lax.broadcasted_iota(jnp.int32, (48, 512), 0) + at_ref[1] * 32 - 8
    y_in = ((y >= 0) & (y < 128)).astype(F32)

    def x_in(x):
        gx = at_ref[0] * 8 + x - 3
        return jnp.where((gx >= 0) & (gx < N_GX * 8), 1.0, 0.0).astype(F32)

    def start(x, carry):
        g = pseudo_weight / (6.0 + gain[x]) * (y_in * x_in(x))
        gain[x] = g
        pa[x] = g * src[x]
        return carry

    lax.fori_loop(0, 14, start, 0)

    def new_row(p, x):
        c = p[x]
        n = p[x - 1] + p[x + 1] + pltpu.roll(c, 1, 0) + pltpu.roll(c, 47, 0)
        n = n + jnp.where(lane == 0, 0.0, pltpu.roll(c, 1, 1))
        n = n + jnp.where(lane == 511, 0.0, pltpu.roll(c, 511, 1))
        return (1.0 - pseudo_weight) * c + gain[x] * (src[x] + n)

    def second(x, carry):
        pb[x] = new_row(pa, x)
        return carry

    lax.fori_loop(1, 13, second, 0)

    def add_source(x, carry):
        src[x, :, 0:128] = src[x, :, 0:128] + ws_ref[x]
        return carry

    lax.fori_loop(2, 12, add_source, 0)

    def third(x, carry):
        pa[x] = new_row(pb, x)
        return carry

    lax.fori_loop(2, 12, third, 0)

    def fourth(x, carry):
        out_ref[x - 3] = new_row(pa, x)[8:40]
        return carry

    lax.fori_loop(3, 11, fourth, 0)


def fluid(at, fs, fd, xa, xb, sib, mid, ws):
    return pl.pallas_call(
        fluid_body,
        out_shape=jax.ShapeDtypeStruct((8, 32, 512), F32),
        in_specs=[SM] + [VM] * 7,
        out_specs=VM,
        scratch_shapes=[pltpu.VMEM((14, 48, 512), F32)] * 4,
        compiler_params=params(),
        cost_estimate=pl.CostEstimate(flops=10**8, bytes_accessed=20 * 10**6, transcendentals=0),
    )(at, fs, fd, xa, xb, sib, mid, ws)


def last_body(s1_ref, got_ref, stiff_ref, f1_ref, w1_ref, f2_ref, w2_ref, out_ref):
    c0, c1 = weights_of(s1_ref[0:1, :], stiff_ref)
    d0, d1 = weights_of(got_ref[...].sum(axis=0, keepdims=True), stiff_ref)
    for c in range(3):
        before = relax_weight * (c0 * f1_ref[c] + c1 * w1_ref[c])
        solved = d0 * f2_ref[c] + d1 * w2_ref[c]
        new = before + relax_weight * (solved - before)
        for r in range(12):
            out_ref[c : c + 1, r * 256 : r * 256 + 256] = new[r : r + 1, :]


def last(s1, got, stiff, f1, w1, f2, w2):
    return pl.pallas_call(
        last_body,
        out_shape=jax.ShapeDtypeStruct((3, 3072), F32),
        in_specs=[VM] * 7,
        out_specs=VM,
        compiler_params=params(),
    )(s1, got, stiff, f1, w1, f2, w2)


def local(
    fluid_source,
    fluid_diag,
    stiff_ref,
    elem_coef,
    connect,
    live_count,
    node_mass,
    solid_load,
    wet_normal,
    trac_face,
    trac_weight,
    wall_node,
    wall_weight,
):
    gx = lax.axis_index("gx")
    gy = lax.axis_index("gy")
    core = gy & 1
    yhi = gy >> 1
    at = jnp.stack([gx, gy]).astype(jnp.int32)

    def in_order(bit, own, other):
        return jnp.concatenate([jnp.where(bit == 0, own, other), jnp.where(bit == 0, other, own)], axis=0)

    even = gx % 2 == 0
    low_pairs = [(i, i ^ 1) for i in range(N_GX)]
    high_pairs = [(i, i + 1) for i in range(1, N_GX - 1, 2)]
    high_pairs = high_pairs + [(j, i) for i, j in high_pairs]

    def beside(to_low, to_high, cross=False):
        sends = jnp.where(even, to_high, to_low), jnp.where(even, to_low, to_high)
        got = []
        for send, pairs in zip(sends, (low_pairs, high_pairs)):
            if cross:
                both_ends = [(4 * i + g, 4 * j + (g ^ (2 * (g & 1)))) for i, j in pairs for g in range(4)]
                got.append(lax.ppermute(send, AXES, both_ends))
            else:
                got.append(lax.ppermute(send, "gx", pairs))
        return got

    def three(part):
        return jnp.stack([fluid_source[part], fluid_diag[part]])

    sa, sb = beside(three(slice(0, 3))[..., :128], three(slice(5, 8))[..., :128])

    own = pack_parts(
        stiff_ref, solid_load, node_mass.reshape(1, 3072), trac_face, trac_weight, wet_normal
    )
    wide = pack_wall(at, fluid_source, fluid_diag, sa, sb, wall_node, wall_weight)
    near = swap(jnp.concatenate([own, wide], axis=0), CORE)
    pair = jnp.concatenate([in_order(core, own, near[:128]), wide + near[128:]], axis=0)
    far = swap(pair, YHI)
    wide = pair[256:] + far[256:]
    slab, pick = wide[:128], wide[128:]
    parts = in_order(yhi, pair[:256], far[:256]).reshape(4, 2, 64, 128)
    parts = jnp.concatenate([parts[:, 0], parts[:, 1]], axis=2)
    seg = parts[:, 48:64]
    load = parts[:, :36].reshape(4, 3, 12, 256).transpose(1, 0, 2, 3).reshape(3, OWN, 256)
    load = jnp.pad(load, ((0, 0), (0, VR - OWN), (0, 0)))
    mass = jnp.pad(parts[:, 36:48].reshape(OWN, 256), ((0, VR - OWN), (0, 0)))
    coef = elem_coef.reshape(1, 384)
    row = lax.broadcasted_iota(jnp.int32, (3, VR, 256), 1)

    def to_all(x):
        return lax.all_to_all(x, AXES, 0, 0, tiled=True)

    def exchange(s):
        pair = s + swap(s, CORE)
        far = swap(pair, YHI)
        ab = beside(pair[:, 0, :], pair[:, OWN, :], cross=True)
        return pair, far, ab

    def edges(far, ab):
        far, (a, b) = lax.optimization_barrier((far, ab))
        got = jnp.stack([jnp.where(even, b, a), jnp.where(even, a, b)])
        return far, got + swap(got, CORE)

    f1 = first_force(at, slab, load, seg)
    following = from_gx(jnp.concatenate([f1[:, 0, :], mass[0:1]], axis=0), -1)
    f1 = jnp.where(row == OWN, following[0:3, None, :], f1)
    mass = jnp.where(row[0] == OWN, following[3:4], mass)

    pair1, far1, ab = exchange(stiff_apply(live_count, f1, connect, coef, stiff_ref))
    far1, edge1 = edges(far1, ab)
    w1, out1, wsb = settle(
        at, live_count, pair1, far1, edge1, mass, f1, connect, coef, stiff_ref, (seg, pick)
    )
    rows, out1 = lax.optimization_barrier(((three(slice(0, 3)), three(slice(5, 8))), out1))
    got1 = to_all(out1)
    xa, xb = beside(*rows)
    f2, ws, s1 = second_force(at, got1, stiff_ref, wsb, slab, load, seg)
    following = from_gx(f2[:, 0, :], -1)
    f2 = jnp.where(row == OWN, following[:, None, :], f2)
    f2, xa, xb = lax.optimization_barrier((f2, xa, xb))
    pair2, far2, ab = exchange(stiff_apply(live_count, f2, connect, coef, stiff_ref))

    xlo, xhi = jnp.where(even, xb, xa), jnp.where(even, xa, xb)

    def columns(part):
        middle = jnp.stack([fluid_source[:, part], fluid_diag[:, part]])
        return jnp.concatenate([xlo[:, :, part], middle, xhi[:, :, part]], axis=1)

    low, high = columns(slice(0, 4)), columns(slice(28, 32))
    sides = (jnp.where(core == 0, high, low), jnp.where(core == 0, low, high))
    padded = jnp.pad(ws, ((0, 0), (8, 8)))
    wall = lax.dynamic_slice_in_dim(padded, gy * 32, 48, axis=1)
    lane = lax.broadcasted_iota(jnp.int32, (16, 48, 128), 2)
    wall = jnp.where(lane == 0, wall[:, :, None], 0.0)
    sides, wall, pair2 = lax.optimization_barrier((sides, wall, pair2))
    far2, edge2 = edges(far2, ab)
    sides, far2, edge2 = lax.optimization_barrier((sides, far2, edge2))
    sib = swap(sides[0], CORE)
    mid = lax.ppermute(sides[1], "gy", [(1, 2), (2, 1)])
    w2, out2 = settle(at, live_count, pair2, far2, edge2, mass, f2, connect, coef, stiff_ref)
    out2, sib, mid = lax.optimization_barrier((out2, sib, mid))
    got2 = to_all(out2)
    pressure = fluid(at, fluid_source, fluid_diag, xa, xb, sib, mid, wall)

    def mine(x):
        return lax.dynamic_slice_in_dim(x, gy * 12, 12, axis=1)

    displacement = last(s1, got2, stiff_ref, mine(f1), mine(w1), mine(f2), mine(w2))
    return pressure, displacement


def solution(mesh):
    in_specs = (
        P("gx", "gy", None),
        P("gx", "gy", None),
        P(),
        P(("gx", "gy")),
        P(None, ("gx", "gy")),
        P(("gx", "gy")),
        P(("gx", "gy")),
        P(None, ("gx", "gy")),
        P(None, ("gx", "gy")),
        P(None, ("gx", "gy")),
        P(None, ("gx", "gy")),
        P(None, "gx", "gy"),
        P(None, "gx", "gy"),
    )
    out_specs = (P("gx", "gy", None), P(None, ("gx", "gy")))
    return jax.shard_map(local, mesh=mesh, in_specs=in_specs, out_specs=out_specs, check_vma=False)
```

```python
import functools

import jax
import jax.numpy as jnp
from jax import lax
from jax.experimental import pallas as pl
from jax.experimental.pallas import tpu as pltpu
from jax.sharding import PartitionSpec as P

F32 = jnp.float32
BF = jnp.bfloat16
AXES = ("gx", "gy")
N_GX = 32
N_DEV = 128
LR = 64
VR = 56
OWN = 48
CORE = 1
YHI = 2

pseudo_weight = 0.8
traction_scale = 30.0
motion_scale = 2.0
relax_weight = 0.5

VM = pl.BlockSpec(memory_space=pltpu.VMEM)
SM = pl.BlockSpec(memory_space=pltpu.SMEM)


def params(mib=40):
    return pltpu.CompilerParams(vmem_limit_bytes=mib << 20)


def swap(x, mask):
    return lax.ppermute(x, AXES, [(i, i ^ mask) for i in range(N_DEV)])


def from_gx(x, by):
    return lax.ppermute(x, "gx", [(i, i + by) for i in range(N_GX) if 0 <= i + by < N_GX])


def from_gy(x, by):
    return lax.ppermute(x, "gy", [(i, i + by) for i in range(4) if 0 <= i + by < 4])


def split(v):
    hi = v.astype(BF)
    return hi, (v - hi.astype(F32)).astype(BF)


def scale_of(stiff_ref):
    r = lax.broadcasted_iota(jnp.int32, (81, 81), 0)
    c = lax.broadcasted_iota(jnp.int32, (81, 81), 1)
    diag = jnp.where(r == c, stiff_ref[...], 0.0)
    trace = diag.sum(axis=1, keepdims=True).sum(axis=0, keepdims=True)
    return 1.0 / jnp.maximum(1.0, trace)


def fill_stiff(stiff_ref, s_scr):
    s_scr[...] = jnp.zeros_like(s_scr)
    hi, lo = split(jnp.pad(stiff_ref[...] * scale_of(stiff_ref), ((0, 15), (0, 7))))
    s_scr[0:96, :] = hi
    s_scr[96:192, :] = lo


def fill_table(v_ref, t_scr):
    blocks = [v_ref[c, 0:OWN, :] for c in range(3)] + [v_ref[c, OWN : OWN + 1, :] for c in range(3)]
    hi, lo = split(jnp.concatenate(blocks + [jnp.zeros((13, 256), F32)], axis=0))
    t_scr[:, 0:256] = hi
    t_scr[:, 256:512] = lo


def select_rows(g, m, c):
    s = (g[c * OWN : (c + 1) * OWN] * m[:OWN]).sum(axis=0, keepdims=True)
    return s + g[144 + c : 145 + c] * m[OWN : OWN + 1]


def block_of(b):
    return pl.ds(pl.multiple_of(b * 128, 128), 128)


def forces_of(x, s_scr, coef_ref, live, b):
    xh, xl = split(x)
    r = jnp.dot(s_scr[...], xh, preferred_element_type=F32)
    prod = r[:88] + r[96:184] + jnp.dot(s_scr[0:96, :], xl, preferred_element_type=F32)[:88]
    slot = lax.broadcasted_iota(jnp.int32, (1, 128), 1) + b * 128
    return prod * jnp.where(slot < live, coef_ref[:, block_of(b)], 0.0)


def apply_body(live_ref, v_ref, conn_ref, coef_ref, stiff_ref, out_ref, t_scr, s_scr, oh_scr, ml_scr, x_scr, a_scr, acc):
    fill_table(v_ref, t_scr)
    fill_stiff(stiff_ref, s_scr)
    x_scr[80:88, :] = jnp.zeros((8, 128), F32)
    acc[...] = jnp.zeros_like(acc)
    b256 = lax.broadcasted_iota(jnp.int32, (256, 128), 0).astype(F32).astype(BF)
    b64 = b256[:LR]
    one, nil = jnp.ones((256, 128), BF), jnp.zeros((256, 128), BF)
    oh_scr[:, 27 * 128 :] = jnp.zeros((256, 128), BF)
    ml_scr[:, 27 * 128 :] = jnp.zeros((LR, 128), BF)
    a_scr[:, 27 * 128 :] = jnp.zeros((320, 128), BF)
    live = live_ref[0]

    def block(b, carry):
        for p in range(14):
            for h in range(2):
                k = 2 * p + h
                if k < 27:
                    sl = slice(k * 128, k * 128 + 128)
                    idx = conn_ref[k : k + 1, block_of(b)]
                    oh_scr[:, sl] = jnp.where(b256 == (idx & 255).astype(F32).astype(BF), one, nil)
                    ml_scr[:, sl] = jnp.where(b64 == (idx >> 8).astype(F32).astype(BF), one[:LR], nil[:LR])
            sp = slice(p * 256, p * 256 + 256)
            oh = oh_scr[:, sp]
            g = jnp.dot(t_scr[...], jnp.concatenate([oh, oh], axis=0), preferred_element_type=F32)
            m = ml_scr[:, sp].astype(F32)
            for c in range(3):
                s = select_rows(g, m, c)
                for h in range(2):
                    k = 2 * p + h
                    if k < 27:
                        x_scr[c * 27 + k : c * 27 + k + 1, :] = s[:, h * 128 : h * 128 + 128]
        prod = forces_of(x_scr[...], s_scr, coef_ref, live, b)
        ph = prod.astype(BF).astype(F32)
        parts = (ph, prod - ph)
        for k in range(27):
            sl = slice(k * 128, k * 128 + 128)
            m = ml_scr[0:OWN, sl].reshape(3, 16, 128)
            last_row = ml_scr[OWN : OWN + 16, sl].astype(F32)[0:1]
            for j, src in enumerate(parts):
                rows = [src[c * 27 + k : c * 27 + k + 1, :] for c in range(3)]
                for c in range(3):
                    r16 = jnp.broadcast_to(rows[c], (16, 128)).astype(BF)
                    at = j * 160 + c * OWN
                    a_scr[at : at + OWN, sl] = (m * r16[None]).reshape(OWN, 128)
                tail = jnp.concatenate(rows + [jnp.zeros((13, 128), F32)], axis=0) * last_row
                a_scr[j * 160 + 144 : j * 160 + 160, sl] = tail.astype(BF)
        acc[...] += lax.dot_general(
            a_scr[...], oh_scr[...], (((1,), (1,)), ((), ())), preferred_element_type=F32
        )
        return carry

    lax.fori_loop(0, (live + 127) // 128, block, 0)
    for c in range(3):
        at = c * OWN
        out_ref[c, 0:OWN, :] = acc[at : at + OWN, :] + acc[160 + at : 160 + at + OWN, :]
        tail = acc[144 + c : 145 + c, :] + acc[304 + c : 305 + c, :]
        out_ref[c, OWN:VR, :] = jnp.concatenate([tail, jnp.zeros((VR - OWN - 1, 256), F32)], axis=0)


def stiff_apply(live, v, conn, coef, stiff):
    return pl.pallas_call(
        apply_body,
        out_shape=jax.ShapeDtypeStruct((3, VR, 256), F32),
        in_specs=[SM] + [VM] * 4,
        out_specs=VM,
        scratch_shapes=[
            pltpu.VMEM((160, 512), BF),
            pltpu.VMEM((192, 88), BF),
            pltpu.VMEM((256, 3584), BF),
            pltpu.VMEM((LR, 3584), BF),
            pltpu.VMEM((88, 128), F32),
            pltpu.VMEM((320, 3584), BF),
            pltpu.VMEM((320, 256), F32),
        ],
        compiler_params=params(),
        cost_estimate=pl.CostEstimate(flops=6 * 10**9, bytes_accessed=24 * 10**6, transcendentals=0),
    )(live, v, conn, coef, stiff)


def pack_parts_body(stiff_ref, load_ref, mass_ref, face_ref, tw_ref, normal_ref, out_ref):
    def put(at, row):
        out_ref[at : at + 1, :] = row[:, :128]
        out_ref[64 + at : 65 + at, :] = row[:, 128:]

    scale = scale_of(stiff_ref)
    for r in range(12):
        sl = slice(r * 256, r * 256 + 256)
        for c in range(3):
            put(c * 12 + r, load_ref[c : c + 1, sl])
        put(36 + r, mass_ref[:, sl] * scale)
    for k in range(4):
        put(48 + k, face_ref[k : k + 1, :].astype(F32))
        put(52 + k, tw_ref[k : k + 1, :])
    for c in range(3):
        put(56 + c, normal_ref[c : c + 1, :])
    zero = jnp.zeros((1, 256), F32)
    for r in range(59, 64):
        put(r, zero)


def pack_parts(stiff, load, mass, face, weight, normal):
    return pl.pallas_call(
        pack_parts_body,
        out_shape=jax.ShapeDtypeStruct((128, 128), F32),
        in_specs=[VM] * 6,
        out_specs=VM,
        compiler_params=params(),
    )(stiff, load, mass, face, weight, normal)


def pack_wall_body(at_ref, fs_ref, fd_ref, xa_ref, xb_ref, node_ref, ww_ref, out_ref):
    out_ref[...] = jnp.zeros_like(out_ref)
    even = jnp.full((32, 128), at_ref[0] & 1, jnp.int32) == 0
    for j, ref in enumerate((fs_ref, fd_ref)):
        for x in range(14):
            if x < 3:
                v = jnp.where(even, xb_ref[j, x], xa_ref[j, x])
            elif x < 11:
                v = ref[x - 3]
            else:
                v = jnp.where(even, xa_ref[j, x - 11], xb_ref[j, x - 11])
            t = v.T
            for z in range(4):
                at = j * 64 + z * 16 + x
                out_ref[at : at + 1, 0:32] = t[z : z + 1, :]
    for k in range(4):
        out_ref[128 + k * 8 : 136 + k * 8, 0:32] = node_ref[k].astype(F32)
        out_ref[160 + k * 8 : 168 + k * 8, 0:32] = ww_ref[k]
    out_ref[...] = pltpu.roll(out_ref[...], at_ref[1] * 32, 1)


def pack_wall(at, fs, fd, xa, xb, node, weight):
    def block(*shape):
        return pl.BlockSpec(shape, lambda i: (0,) * len(shape))

    return pl.pallas_call(
        pack_wall_body,
        grid=(1,),
        out_shape=jax.ShapeDtypeStruct((192, 128), F32),
        in_specs=[
            SM,
            block(8, 32, 128),
            block(8, 32, 128),
            block(2, 3, 32, 128),
            block(2, 3, 32, 128),
            block(4, 8, 32),
            block(4, 8, 32),
        ],
        out_specs=block(192, 128),
        compiler_params=params(),
    )(at, fs, fd, xa, xb, node, weight)


def source_of(vec_ref, seg_ref, pick_ref):
    rows = []
    for g in range(4):
        total = jnp.zeros((1, 256), F32)
        for c in range(3):
            total = total + seg_ref[g, 8 + c : 9 + c, :] * vec_ref[c, 12 * g : 12 * g + 1, :]
        rows.append(total)
    return split(jnp.concatenate(rows + [jnp.zeros((4, 256), F32)], axis=0))


def settle_body(*refs, first):
    at_ref, live_ref, p_ref, q_ref, edge_ref, mass_ref, v_ref, conn_ref, coef_ref, stiff_ref = refs[:10]
    if first:
        seg_ref, pick_ref, w_ref, out_ref, ws_ref = refs[10:15]
    else:
        w_ref, out_ref = refs[10:12]
    t_scr, s_scr, x_scr, acc = refs[-4:]
    keep = lax.broadcasted_iota(jnp.int32, (VR, 256), 0)
    end = jnp.where(at_ref[0] == N_GX - 1, OWN, OWN + 1)
    mask = (keep < end).astype(F32)
    mass = mass_ref[...]
    dots = [jnp.zeros((8, 256), F32) for _ in range(4)]
    for c in range(3):
        v = v_ref[c]
        w = p_ref[c] + q_ref[c]
        w = w + jnp.where(keep == 0, edge_ref[0, c : c + 1, :], jnp.where(keep == OWN, edge_ref[1, c : c + 1, :], 0.0))
        w = (w + mass * v) * mask
        w_ref[c] = w
        for i, (x, y) in enumerate(((v, v), (v, w), (w, w), (w, mass * w))):
            dots[i] = dots[i] + (x[:OWN] * y[:OWN]).reshape(6, 8, 256).sum(axis=0)
    dots = [0.25 * d.sum(axis=0, keepdims=True).sum(axis=1, keepdims=True) for d in dots]

    if first:
        hf, lf = source_of(v_ref, seg_ref, pick_ref)
        hw, lw = source_of(w_ref, seg_ref, pick_ref)
        table = jnp.concatenate([hf, lf, hw, lw], axis=0)
        n256 = lax.broadcasted_iota(jnp.int32, (256, 128), 0).astype(F32).astype(BF)
        unit, none = jnp.ones((256, 128), BF), jnp.zeros((256, 128), BF)
        n8 = lax.broadcasted_iota(jnp.int32, (8, 128), 0)
        for x in range(8):
            tf = jnp.zeros((8, 128), F32)
            tw = jnp.zeros((8, 128), F32)
            for k in range(4):
                row = k * 8 + x
                node = pick_ref[row : row + 1, :].astype(jnp.int32)
                oh = jnp.where(n256 == (node & 255).astype(F32).astype(BF), unit, none)
                r = jnp.dot(table, oh, preferred_element_type=F32)
                u = jnp.where(n8 == (node >> 8), pick_ref[32 + row : 33 + row, :], 0.0)
                tf = tf + (r[0:8] + r[8:16]) * u
                tw = tw + (r[16:24] + r[24:32]) * u
            ws_ref[x : x + 1, :] = (motion_scale * relax_weight) * tf.sum(axis=0, keepdims=True)
            ws_ref[8 + x : 9 + x, :] = (motion_scale * relax_weight) * tw.sum(axis=0, keepdims=True)

    fill_table(w_ref, t_scr)
    fill_stiff(stiff_ref, s_scr)
    acc[...] = jnp.zeros_like(acc)
    x_scr[80:88, :] = jnp.zeros((8, 128), F32)
    b256 = lax.broadcasted_iota(jnp.int32, (256, 128), 0).astype(F32).astype(BF)
    one, nil = jnp.ones((256, 128), BF), jnp.zeros((256, 128), BF)
    i64 = lax.broadcasted_iota(jnp.int32, (LR, 128), 0)
    live = live_ref[0]

    def block(b, carry):
        for p in range(14):
            pieces, masks = [], []
            for k in (2 * p, 2 * p + 1):
                idx = conn_ref[min(k, 26) : min(k, 26) + 1, block_of(b)]
                pieces.append(jnp.where(b256 == (idx & 255).astype(F32).astype(BF), one, nil))
                masks.append((i64 == (idx >> 8)).astype(F32))
            oh = jnp.concatenate(pieces, axis=1)
            g = jnp.dot(t_scr[...], jnp.concatenate([oh, oh], axis=0), preferred_element_type=F32)
            m = jnp.concatenate(masks, axis=1)
            for c in range(3):
                s = select_rows(g, m, c)
                for h in range(2):
                    k = 2 * p + h
                    if k < 27:
                        x_scr[c * 27 + k : c * 27 + k + 1, :] = s[:, h * 128 : h * 128 + 128]
        x = x_scr[...]
        acc[...] += (forces_of(x, s_scr, coef_ref, live, b) * x).sum(axis=0, keepdims=True)
        return carry

    lax.fori_loop(0, (live + 127) // 128, block, 0)
    dots[3] = dots[3] + acc[...].sum(axis=1, keepdims=True)
    lane = lax.broadcasted_iota(jnp.int32, (1, 128), 1)
    row = jnp.zeros((1, 128), F32)
    for i in range(4):
        row = jnp.where(lane == i, dots[i], row)
    row = jnp.broadcast_to(row, (N_DEV, 128))
    if first:
        peer = lax.broadcasted_iota(jnp.int32, (N_DEV, 128), 0) >> 2
        after = peer > at_ref[0]
        out_ref[pl.ds(0, N_DEV, 4), :] = row
        out_ref[pl.ds(1, N_DEV, 4), :] = jnp.where(after, ws_ref[7:8, :], ws_ref[0:1, :])
        out_ref[pl.ds(2, N_DEV, 4), :] = jnp.where(after, ws_ref[15:16, :], ws_ref[8:9, :])
        out_ref[pl.ds(3, N_DEV, 4), :] = jnp.zeros((N_DEV, 128), F32)
    else:
        out_ref[...] = row


def settle(at, live, p, q, edge, mass, v, conn, coef, stiff, wall=()):
    first = bool(wall)
    shapes = [(3, VR, 256), (4 * N_DEV, 128), (16, 128)] if first else [(3, VR, 256), (N_DEV, 128)]
    return pl.pallas_call(
        functools.partial(settle_body, first=first),
        out_shape=tuple(jax.ShapeDtypeStruct(x, F32) for x in shapes),
        in_specs=[SM, SM] + [VM] * (8 + len(wall)),
        out_specs=(VM,) * len(shapes),
        scratch_shapes=[
            pltpu.VMEM((160, 512), BF),
            pltpu.VMEM((192, 88), BF),
            pltpu.VMEM((88, 128), F32),
            pltpu.VMEM((1, 128), F32),
        ],
        compiler_params=params(),
        cost_estimate=pl.CostEstimate(flops=6 * 10**9, bytes_accessed=24 * 10**6, transcendentals=0),
    )(at, live, p, q, edge, mass, v, conn, coef, stiff, *wall)


def rows_in(at_ref):
    x = lax.broadcasted_iota(jnp.int32, (16, 128), 0) + at_ref[0] * 8 - 3
    return ((x >= 0) & (x < N_GX * 8)).astype(F32)


def wall_step(p, gain, force, inside, depth):
    lane = lax.broadcasted_iota(jnp.int32, (16, 128), 1)
    out = []
    for z in range(depth):
        c = p[z]
        n = pltpu.roll(c, 1, 0) + pltpu.roll(c, 15, 0)
        n = n + jnp.where(lane == 0, 0.0, pltpu.roll(c, 1, 1))
        n = n + jnp.where(lane == 127, 0.0, pltpu.roll(c, 127, 1))
        n = n + p[z + 1]
        if z > 0:
            n = n + p[z - 1]
        out.append(((1.0 - pseudo_weight) * c + gain[z] * (force[z] + n)) * inside)
    return out


def wall_front(at_ref, slab_ref):
    inside = rows_in(at_ref)
    fs = [slab_ref[z * 16 : z * 16 + 16, :] for z in range(4)]
    gain = [pseudo_weight / (6.0 + slab_ref[64 + z * 16 : 64 + z * 16 + 16, :]) for z in range(4)]
    p1 = [gain[z] * fs[z] * inside for z in range(4)]
    p2 = wall_step(p1, gain, fs, inside, 3)
    return inside, fs, gain, p2


def push(wall16, load_ref, seg_ref, f_ref):
    wall = pltpu.roll(wall16, 13, 0)[0:8]
    hi, lo = split(wall)
    table = jnp.concatenate([hi, lo], axis=0)
    b128 = lax.broadcasted_iota(jnp.int32, (128, 256), 0).astype(F32).astype(BF)
    one, nil = jnp.ones((128, 256), BF), jnp.zeros((128, 256), BF)
    i8 = lax.broadcasted_iota(jnp.int32, (8, 256), 0)
    f_ref[...] = load_ref[...]
    for g in range(4):
        total = jnp.zeros((8, 256), F32)
        for k in range(4):
            face = seg_ref[g, k : k + 1, :].astype(jnp.int32)
            lane = (face >> 8) * 32 + (face & 31)
            oh = jnp.where(b128 == lane.astype(F32).astype(BF), one, nil)
            r = jnp.dot(table, oh, preferred_element_type=F32)
            w = jnp.where(i8 == ((face >> 5) & 7), seg_ref[g, 4 + k : 5 + k, :], 0.0)
            total = total + (r[:8] + r[8:]) * w
        traction = total.sum(axis=0, keepdims=True)
        for c in range(3):
            f_ref[c, 12 * g : 12 * g + 1, :] = (
                f_ref[c, 12 * g : 12 * g + 1, :]
                + traction_scale * traction * seg_ref[g, 8 + c : 9 + c, :]
            )


def first_body(at_ref, slab_ref, load_ref, seg_ref, f_ref):
    inside, fs, gain, p2 = wall_front(at_ref, slab_ref)
    push(p2[0], load_ref, seg_ref, f_ref)


def first_force(at, slab, load, seg):
    return pl.pallas_call(
        first_body,
        out_shape=jax.ShapeDtypeStruct((3, VR, 256), F32),
        in_specs=[SM, VM, VM, VM],
        out_specs=VM,
        compiler_params=params(),
    )(at, slab, load, seg)


def weights_of(sums, stiff_ref):
    lane = lax.broadcasted_iota(jnp.int32, (1, 128), 1)
    a, b, c, d = [jnp.where(lane == i, sums, 0.0).sum(axis=1, keepdims=True) for i in range(4)]
    inv = scale_of(stiff_ref)
    alpha = a / b
    beta = (c - b * (b / a)) / (d - c * (c / b))
    return (alpha + beta * (alpha * (c / b))) * inv, -(alpha * beta) * inv


def second_body(at_ref, got_ref, stiff_ref, ws_ref, slab_ref, load_ref, seg_ref, f_ref, wall_ref, sums_ref):
    inside, fs, gain, p2 = wall_front(at_ref, slab_ref)
    sums = got_ref[pl.ds(0, N_DEV, 4), :].sum(axis=0, keepdims=True)
    sums_ref[...] = jnp.broadcast_to(sums, (8, 128))
    c0, c1 = weights_of(sums, stiff_ref)
    gx = at_ref[0]
    wall_ref[...] = jnp.zeros_like(wall_ref)
    wall_ref[3:11, :] = c0 * ws_ref[0:8, :] + c1 * ws_ref[8:16, :]
    for row, by, edge in ((2, -1, 0), (11, 1, N_GX - 1)):
        peer = jnp.clip(gx + by, 0, N_GX - 1) * 4 + at_ref[1]
        got = c0 * got_ref[pl.ds(peer * 4 + 1, 1), :] + c1 * got_ref[pl.ds(peer * 4 + 2, 1), :]
        wall_ref[row : row + 1, :] = jnp.where(jnp.full((1, 128), gx, jnp.int32) == edge, 0.0, got)
    force = [fs[0] + wall_ref[...], fs[1]]
    p3 = wall_step(p2, gain, force, inside, 2)
    p4 = wall_step(p3, gain, force, inside, 1)
    push(p4[0], load_ref, seg_ref, f_ref)


def second_force(at, got, stiff, ws, slab, load, seg):
    return pl.pallas_call(
        second_body,
        out_shape=(
            jax.ShapeDtypeStruct((3, VR, 256), F32),
            jax.ShapeDtypeStruct((16, 128), F32),
            jax.ShapeDtypeStruct((8, 128), F32),
        ),
        in_specs=[SM] + [VM] * 6,
        out_specs=(VM, VM, VM),
        compiler_params=params(),
    )(at, got, stiff, ws, slab, load, seg)


def fluid_body(at_ref, fs_ref, fd_ref, xa_ref, xb_ref, sib_ref, mid_ref, ws_ref, out_ref, src, gain, pa, pb):
    odd = jnp.full((4, 512), at_ref[1] & 1, jnp.int32) == 1
    even = jnp.full((32, 512), at_ref[0] & 1, jnp.int32) == 0
    zero = jnp.zeros((4, 512), F32)
    for j, (ref, dst) in enumerate(((fs_ref, src), (fd_ref, gain))):
        for x in range(14):
            if x < 3:
                own = jnp.where(even, xb_ref[j, x], xa_ref[j, x])
            elif x < 11:
                own = ref[x - 3]
            else:
                own = jnp.where(even, xa_ref[j, x - 11], xb_ref[j, x - 11])
            dst[x, 8:40, :] = own
            sib, mid = sib_ref[j, x], mid_ref[j, x]
            dst[x, 0:8, :] = jnp.concatenate([zero, jnp.where(odd, sib, mid)], axis=0)
            dst[x, 40:48, :] = jnp.concatenate([jnp.where(odd, mid, sib), zero], axis=0)
    lane = lax.broadcasted_iota(jnp.int32, (48, 512), 1)
    y = lax.broadcasted_iota(jnp.int32, (48, 512), 0) + at_ref[1] * 32 - 8
    y_in = ((y >= 0) & (y < 128)).astype(F32)

    def x_in(x):
        gx = at_ref[0] * 8 + x - 3
        return jnp.where((gx >= 0) & (gx < N_GX * 8), 1.0, 0.0).astype(F32)

    def start(x, carry):
        g = pseudo_weight / (6.0 + gain[x]) * (y_in * x_in(x))
        gain[x] = g
        pa[x] = g * src[x]
        return carry

    lax.fori_loop(0, 14, start, 0)

    def new_row(p, x):
        c = p[x]
        n = p[x - 1] + p[x + 1] + pltpu.roll(c, 1, 0) + pltpu.roll(c, 47, 0)
        n = n + jnp.where(lane == 0, 0.0, pltpu.roll(c, 1, 1))
        n = n + jnp.where(lane == 511, 0.0, pltpu.roll(c, 511, 1))
        return (1.0 - pseudo_weight) * c + gain[x] * (src[x] + n)

    def second(x, carry):
        pb[x] = new_row(pa, x)
        return carry

    lax.fori_loop(1, 13, second, 0)

    def add_source(x, carry):
        src[x, :, 0:128] = src[x, :, 0:128] + ws_ref[x]
        return carry

    lax.fori_loop(2, 12, add_source, 0)

    def third(x, carry):
        pa[x] = new_row(pb, x)
        return carry

    lax.fori_loop(2, 12, third, 0)

    def fourth(x, carry):
        out_ref[x - 3] = new_row(pa, x)[8:40]
        return carry

    lax.fori_loop(3, 11, fourth, 0)


def fluid(at, fs, fd, xa, xb, sib, mid, ws):
    return pl.pallas_call(
        fluid_body,
        out_shape=jax.ShapeDtypeStruct((8, 32, 512), F32),
        in_specs=[SM] + [VM] * 7,
        out_specs=VM,
        scratch_shapes=[pltpu.VMEM((14, 48, 512), F32)] * 4,
        compiler_params=params(),
        cost_estimate=pl.CostEstimate(flops=10**8, bytes_accessed=20 * 10**6, transcendentals=0),
    )(at, fs, fd, xa, xb, sib, mid, ws)


def last_body(s1_ref, got_ref, stiff_ref, f1_ref, w1_ref, f2_ref, w2_ref, out_ref):
    c0, c1 = weights_of(s1_ref[0:1, :], stiff_ref)
    d0, d1 = weights_of(got_ref[...].sum(axis=0, keepdims=True), stiff_ref)
    for c in range(3):
        before = relax_weight * (c0 * f1_ref[c] + c1 * w1_ref[c])
        solved = d0 * f2_ref[c] + d1 * w2_ref[c]
        new = before + relax_weight * (solved - before)
        for r in range(12):
            out_ref[c : c + 1, r * 256 : r * 256 + 256] = new[r : r + 1, :]


def last(s1, got, stiff, f1, w1, f2, w2):
    return pl.pallas_call(
        last_body,
        out_shape=jax.ShapeDtypeStruct((3, 3072), F32),
        in_specs=[VM] * 7,
        out_specs=VM,
        compiler_params=params(),
    )(s1, got, stiff, f1, w1, f2, w2)


def local(
    fluid_source,
    fluid_diag,
    stiff_ref,
    elem_coef,
    connect,
    live_count,
    node_mass,
    solid_load,
    wet_normal,
    trac_face,
    trac_weight,
    wall_node,
    wall_weight,
):
    gx = lax.axis_index("gx")
    gy = lax.axis_index("gy")
    core = gy & 1
    yhi = gy >> 1
    at = jnp.stack([gx, gy]).astype(jnp.int32)

    def in_order(bit, own, other):
        return jnp.concatenate([jnp.where(bit == 0, own, other), jnp.where(bit == 0, other, own)], axis=0)

    even = gx % 2 == 0
    low_pairs = [(i, i ^ 1) for i in range(N_GX)]
    high_pairs = [(i, i + 1) for i in range(1, N_GX - 1, 2)]
    high_pairs = high_pairs + [(j, i) for i, j in high_pairs]

    def beside(to_low, to_high, cross=False):
        sends = jnp.where(even, to_high, to_low), jnp.where(even, to_low, to_high)
        got = []
        for send, pairs in zip(sends, (low_pairs, high_pairs)):
            if cross:
                both_ends = [(4 * i + g, 4 * j + (g ^ (2 * (g & 1)))) for i, j in pairs for g in range(4)]
                got.append(lax.ppermute(send, AXES, both_ends))
            else:
                got.append(lax.ppermute(send, "gx", pairs))
        return got

    def three(part):
        return jnp.stack([fluid_source[part], fluid_diag[part]])

    sa, sb = beside(three(slice(0, 3))[..., :128], three(slice(5, 8))[..., :128])

    own = pack_parts(
        stiff_ref, solid_load, node_mass.reshape(1, 3072), trac_face, trac_weight, wet_normal
    )
    wide = pack_wall(at, fluid_source, fluid_diag, sa, sb, wall_node, wall_weight)
    near = swap(jnp.concatenate([own, wide], axis=0), CORE)
    pair = jnp.concatenate([in_order(core, own, near[:128]), wide + near[128:]], axis=0)
    far = swap(pair, YHI)
    wide = pair[256:] + far[256:]
    slab, pick = wide[:128], wide[128:]
    parts = in_order(yhi, pair[:256], far[:256]).reshape(4, 2, 64, 128)
    parts = jnp.concatenate([parts[:, 0], parts[:, 1]], axis=2)
    seg = parts[:, 48:64]
    load = parts[:, :36].reshape(4, 3, 12, 256).transpose(1, 0, 2, 3).reshape(3, OWN, 256)
    load = jnp.pad(load, ((0, 0), (0, VR - OWN), (0, 0)))
    mass = jnp.pad(parts[:, 36:48].reshape(OWN, 256), ((0, VR - OWN), (0, 0)))
    coef = elem_coef.reshape(1, 384)
    row = lax.broadcasted_iota(jnp.int32, (3, VR, 256), 1)

    def to_all(x):
        return lax.all_to_all(x, AXES, 0, 0, tiled=True)

    def exchange(s):
        pair = s + swap(s, CORE)
        far = swap(pair, YHI)
        ab = beside(pair[:, 0, :], pair[:, OWN, :], cross=True)
        return pair, far, ab

    def edges(far, ab):
        far, (a, b) = lax.optimization_barrier((far, ab))
        got = jnp.stack([jnp.where(even, b, a), jnp.where(even, a, b)])
        return far, got + swap(got, CORE)

    f1 = first_force(at, slab, load, seg)
    following = from_gx(jnp.concatenate([f1[:, 0, :], mass[0:1]], axis=0), -1)
    f1 = jnp.where(row == OWN, following[0:3, None, :], f1)
    mass = jnp.where(row[0] == OWN, following[3:4], mass)

    pair1, far1, ab = exchange(stiff_apply(live_count, f1, connect, coef, stiff_ref))
    far1, edge1 = edges(far1, ab)
    w1, out1, wsb = settle(
        at, live_count, pair1, far1, edge1, mass, f1, connect, coef, stiff_ref, (seg, pick)
    )
    rows, out1 = lax.optimization_barrier(((three(slice(0, 3)), three(slice(5, 8))), out1))
    got1 = to_all(out1)
    xa, xb = beside(*rows)
    f2, ws, s1 = second_force(at, got1, stiff_ref, wsb, slab, load, seg)
    following = from_gx(f2[:, 0, :], -1)
    f2 = jnp.where(row == OWN, following[:, None, :], f2)
    f2, xa, xb = lax.optimization_barrier((f2, xa, xb))
    pair2, far2, ab = exchange(stiff_apply(live_count, f2, connect, coef, stiff_ref))

    xlo, xhi = jnp.where(even, xb, xa), jnp.where(even, xa, xb)

    def columns(part):
        middle = jnp.stack([fluid_source[:, part], fluid_diag[:, part]])
        return jnp.concatenate([xlo[:, :, part], middle, xhi[:, :, part]], axis=1)

    low, high = columns(slice(0, 4)), columns(slice(28, 32))
    sides = (jnp.where(core == 0, high, low), jnp.where(core == 0, low, high))
    padded = jnp.pad(ws, ((0, 0), (8, 8)))
    wall = lax.dynamic_slice_in_dim(padded, gy * 32, 48, axis=1)
    lane = lax.broadcasted_iota(jnp.int32, (16, 48, 128), 2)
    wall = jnp.where(lane == 0, wall[:, :, None], 0.0)
    sides, wall, pair2 = lax.optimization_barrier((sides, wall, pair2))
    far2, edge2 = edges(far2, ab)
    sides, far2, edge2 = lax.optimization_barrier((sides, far2, edge2))
    sib = swap(sides[0], CORE)
    mid = lax.ppermute(sides[1], "gy", [(1, 2), (2, 1)])
    w2, out2 = settle(at, live_count, pair2, far2, edge2, mass, f2, connect, coef, stiff_ref)
    out2, sib, mid = lax.optimization_barrier((out2, sib, mid))
    got2 = to_all(out2)
    pressure = fluid(at, fluid_source, fluid_diag, xa, xb, sib, mid, wall)

    def mine(x):
        return lax.dynamic_slice_in_dim(x, gy * 12, 12, axis=1)

    displacement = last(s1, got2, stiff_ref, mine(f1), mine(w1), mine(f2), mine(w2))
    return pressure, displacement


def solution(mesh):
    in_specs = (
        P("gx", "gy", None),
        P("gx", "gy", None),
        P(),
        P(("gx", "gy")),
        P(None, ("gx", "gy")),
        P(("gx", "gy")),
        P(("gx", "gy")),
        P(None, ("gx", "gy")),
        P(None, ("gx", "gy")),
        P(None, ("gx", "gy")),
        P(None, ("gx", "gy")),
        P(None, "gx", "gy"),
        P(None, "gx", "gy"),
    )
    out_specs = (P("gx", "gy", None), P(None, ("gx", "gy")))
    return jax.shard_map(local, mesh=mesh, in_specs=in_specs, out_specs=out_specs, check_vma=False)
```
